32 devices in a mesh: dp: 8 (over z, x), tensor: 4 (over y, core).
Axes of the slice: x: 2, y: 2, z: 4, core: 2. Of those that a mesh axis runs over, the one named last changes fastest.
Arguments:
- layer_input: bfloat16 [4096, 768], P(('dp', 'tensor')), may hold values from -6 to 6
- seq_lengths: int32 [8, 3], P('dp'), may hold values from 1 to 480, 512 in all within a row
- expert_ids: int32 [4096, 1], P('dp'), may hold values from 0 to 7; in each aligned block of 512 rows (0 to 511, 512 to 1023, ...) at most 65 rows name the same one
- bucket_table: int32 [959], replicated, may hold values from 0 to 31, as said below
- gain_attn: bfloat16 [768], replicated, may hold values from 0.5 to 1.5
- gain_moe: bfloat16 [768], replicated, may hold values from 0.5 to 1.5
- w_query: bfloat16 [768, 768], P('dp', 'tensor'), may hold values from -0.21875 to 0.21875
- w_key: bfloat16 [768, 768], P('dp', 'tensor'), may hold values from -0.21875 to 0.21875
- w_value: bfloat16 [768, 768], P('dp', 'tensor'), may hold values from -0.21875 to 0.21875
- w_attn_out: bfloat16 [768, 768], P('tensor', 'dp'), may hold values from -3 to 3
- w_router: bfloat16 [768, 8], P('dp'), may hold values from -0.109375 to 0.109375
- rel_bias: bfloat16 [32, 12], P(None, 'tensor'), may hold values from -4 to 4
- w_in: bfloat16 [8, 768, 3072], P('dp', None, 'tensor'), may hold values from -0.21875 to 0.21875
- w_out: bfloat16 [8, 3072, 768], P('dp', 'tensor'), may hold values from -4 to 4
- cotangent: bfloat16 [4096, 768], P(('dp', 'tensor')), may hold values from -6 to 6
Outputs:
- layer_output: bfloat16 [4096, 768], P(('dp', 'tensor'))
- grad_input: float32 [4096, 768], P(('dp', 'tensor'))
- grad_gain_attn: float32 [768], replicated
- grad_gain_moe: float32 [768], replicated
- grad_query: float32 [768, 768], P('dp', 'tensor')
- grad_key: float32 [768, 768], P('dp', 'tensor')
- grad_value: float32 [768, 768], P('dp', 'tensor')
- grad_attn_out: float32 [768, 768], P('tensor', 'dp')
- grad_router: float32 [768, 8], P('dp')
- grad_rel_bias: float32 [32, 12], P(None, 'tensor')
- grad_w_in: float32 [8, 768, 3072], P('dp', None, 'tensor')
- grad_w_out: float32 [8, 3072, 768], P('dp', 'tensor')
The draws below stay inside these ranges and needn't reach their ends.
Inputs may be any that keep to these rules, and one draw needn't show every extreme that they name: `seq_lengths`: row g lists the lengths of the sequences packed, in order, into the 512 tokens of group g; each row sums to 512. `expert_ids`: within the 512 tokens of one group no expert is named by more than 65 tokens. `bucket_table`: entry r is the bucket of the relative position r - 480 + 1 (key position minus query position); it depends only on that position.
All inputs are finite; a program needn't handle non-finite values.
Results may differ from the reference program's by a relative error of at most 0.025.
Values may be sent and summed in bfloat16 or wider, within the bound.
A program may use at most 128 MiB of HBM per device.

```python
import math
import jax
import jax.numpy as jnp
import numpy as np
from jax import lax

D = 768
H = 12
DH = 64
FF = 3072
NB = 32
SEQS = 3
EXPERTS = 8
TOK_GRP = 512
TOKENS = 4096
MAXLEN = 480
CAP = 65
N_DP = 8


def draw_bucket_table(key, part):
    key = jax.random.fold_in(key, 7)
    reach = min(128, MAXLEN)
    near = NB // 4
    count = NB // 2 - near - 1
    choices_len = reach - near - 1
    scores = jax.random.randint(key, (choices_len,), 0, 1 << 20) * choices_len + jnp.arange(choices_len)
    marks = jnp.sort(jnp.argsort(scores)[:count] + near + 1)
    offsets = jnp.arange(2 * MAXLEN - 1) - (MAXLEN - 1)
    distance = jnp.abs(offsets)
    far = near + jnp.sum((distance[:, None] >= marks[None, :]).astype(jnp.int32), axis=1)
    bucket = jnp.where(distance < near, distance, far)
    side = jnp.where(offsets > 0, NB // 2, 0)
    return (bucket + side).astype(jnp.int32)


def steps_of(rng, shape, pieces, least, high):
    factor_of, own = 1.0, jax.random.fold_in(rng, 6)
    for dim, blocks in pieces:
        draws = jnp.exp(jax.random.uniform(jax.random.fold_in(own, dim), (blocks,), jnp.float32, least / len(pieces), high / len(pieces)))
        factor_of = factor_of * jnp.repeat(draws, shape[dim] // blocks).reshape([-1 if axis == dim else 1 for axis in range(len(shape))])
    return factor_of


def profile(count, total, most, slope):
    portions = [(1 << 20) // math.isqrt(grade ** slope) + 1 for grade in range(2, count + 1)]
    surplus, given = total - most - (count - 1), [1] * (count - 1)
    while surplus > 0:
        free = [i for i in range(count - 1) if given[i] < most]
        mass, remaining = sum([portions[i] for i in free]), surplus
        for i in free:
            more = min(most - given[i], max(1, remaining * portions[i] // mass), surplus)
            given[i] = given[i] + more
            surplus = surplus - more
    return np.array([most] + given)


def uneven_parts(key, amount, total, bound, lean):
    if amount == 2:
        one = jax.random.randint(key, (), max(1, total - bound), min(bound, total - 1) + 1)
        return jnp.stack([one, total - one])
    tallies = jnp.asarray(profile(amount, total, bound, lean), jnp.int32)
    twos = (amount - 1) // 2
    giver, taker = tallies[1:1 + 2 * twos:2], tallies[2:2 + 2 * twos:2]
    margin = jnp.minimum(giver - 1, bound - taker)
    passed = jax.random.randint(jax.random.fold_in(key, 1), (twos,), 0, 1 << 20) % (margin + 1)
    tallies = tallies.at[1:1 + 2 * twos:2].set(giver - passed).at[2:2 + 2 * twos:2].set(taker + passed)
    return tallies[jax.random.permutation(jax.random.fold_in(key, 2), amount)]


def shared_out(key, own, number, rows, count, top, bound, slope):
    sequence = jax.random.permutation(key, count)
    heavy_load, usual = portions_of(count, rows * top, bound, slope, True), portions_of(count, rows * top, bound, slope, False)
    places = jnp.arange(count)

    def named(tallies, offset_by):
        used = int((tallies > 0).sum())
        fixed = max(1, used // 4)
        shifted = fixed + (places - fixed + offset_by * (used - fixed)) % max(1, count - fixed)
        return jnp.zeros((count,), jnp.int32).at[sequence[jnp.where(places < fixed, places, shifted)]].set(jnp.asarray(tallies, jnp.int32))

    tallies = jnp.where(number % 4 == 0, named(heavy_load, number // 4), named(usual, number - number // 4 - 1))
    mixed = jax.random.permutation(jax.random.fold_in(own, 3), count)
    giver, receiver = mixed[0:count // 2 * 2:2], mixed[1:count // 2 * 2:2]
    slack = jnp.minimum(tallies[giver] - 1, bound - tallies[receiver]) // 2
    slack = jnp.where((giver == sequence[0]) | (receiver == sequence[0]) | (tallies[receiver] == 0), 0, jnp.maximum(slack, 0))
    shifted = jax.random.randint(jax.random.fold_in(own, 4), (count // 2,), 0, 1 << 20) % (slack + 1)
    tallies = tallies.at[giver].add(-shifted).at[receiver].add(shifted)
    labels = jnp.searchsorted(jnp.cumsum(tallies), jnp.arange(rows * top), side="right").astype(jnp.int32)
    listing = labels.reshape(top, rows).T
    listing = listing[jax.random.permutation(jax.random.fold_in(own, 1), rows)]
    offset_by = jax.random.randint(jax.random.fold_in(own, 2), (rows, 1), 0, top)
    return jnp.take_along_axis(listing, (jnp.arange(top)[None, :] + offset_by) % top, axis=1)


def portions_of(count, total, most, slope, full):
    portions = [(1 << 20) // math.isqrt(grade ** slope) + 1 for grade in range(1, count + 1)]
    largest = most if full else min(most, max(-(-total // count), total * portions[0] // sum(portions)))
    least = 1 if total - largest >= count - 1 else 0
    counts, rest = [largest] + [least] * (count - 1), total - largest - least * (count - 1)
    while rest > 0:
        candidates = [i for i in range(1, count) if counts[i] < largest] or [i for i in range(1, count) if counts[i] < most]
        mass, left = sum([portions[i] for i in candidates]), rest
        for i in candidates:
            extra = min(most - counts[i], max(1, left * portions[i] // mass), rest)
            counts[i] = counts[i] + extra
            rest = rest - extra
    return np.array(counts)


def bell_draw(own_key, extent, width, bound, split=(), held_as=jnp.bfloat16):
    drawn = jax.random.normal(own_key, extent, jnp.float32) * width
    if len(split) > 0:
        drawn = steps_of(own_key, extent, split, -0.22, 0.18) * drawn
    return jnp.clip(drawn, min=-bound, max=bound).astype(held_as)


def setup_inputs(seed: int = 0) -> dict:
    key_list = jax.random.split(jax.random.key(seed), 16)
    layer_input = bell_draw(key_list[0], (TOKENS, D), 1.0, 6.0, ((0, 32),))
    seq_lengths = jax.vmap(lambda own: uneven_parts(own, SEQS, TOK_GRP, MAXLEN, 2))(jax.random.split(key_list[1], N_DP)).reshape((N_DP, SEQS)).astype(jnp.int32)
    expert_ids_keys = jax.random.split(jax.random.fold_in(key_list[2], 1), TOKENS // TOK_GRP)
    expert_ids_turns = jax.random.permutation(jax.random.fold_in(key_list[2], 3), TOKENS // TOK_GRP)
    expert_ids = jax.vmap(lambda own, number: shared_out(jax.random.fold_in(key_list[2], 2), own, number, TOK_GRP, EXPERTS, 1, CAP, 2))(expert_ids_keys, expert_ids_turns).reshape((TOKENS, 1))
    bucket_table = draw_bucket_table(jax.random.fold_in(key_list[15], 71), 0)
    gain_attn = jnp.clip(1.0 + 0.1 * jax.random.normal(key_list[4], (D,), jnp.float32), 0.5, 1.5).astype(jnp.bfloat16)
    gain_moe = jnp.clip(1.0 + 0.1 * jax.random.normal(key_list[5], (D,), jnp.float32), 0.5, 1.5).astype(jnp.bfloat16)
    w_query = bell_draw(key_list[6], (D, H * DH), D ** -0.5, 0.21875, ((0, 8), (1, 4)))
    w_key = bell_draw(key_list[7], (D, H * DH), D ** -0.5, 0.21875, ((0, 8), (1, 4)))
    w_value = bell_draw(key_list[8], (D, H * DH), D ** -0.5, 0.21875, ((0, 8), (1, 4)))
    w_attn_out = bell_draw(key_list[9], (H * DH, D), 4 ** -0.5, 3.0, ((0, 4), (1, 8)))
    w_router = bell_draw(key_list[10], (D, EXPERTS), (4 * D) ** -0.5, 0.109375, ((0, 8),))
    rel_bias = bell_draw(key_list[11], (NB, H), 1.0, 4.0, ((1, 4),))
    w_in = bell_draw(key_list[12], (EXPERTS, D, FF), D ** -0.5, 0.21875, ((0, 8), (2, 4)))
    w_out = bell_draw(key_list[13], (EXPERTS, FF, D), (2 * EXPERTS * FF ** -0.5), 4.0, ((0, 8), (1, 4)))
    cotangent = bell_draw(key_list[14], (TOKENS, D), 1.0, 6.0, ((0, 32),))
    return {"layer_input": layer_input, "seq_lengths": seq_lengths, "expert_ids": expert_ids, "bucket_table": bucket_table, "gain_attn": gain_attn, "gain_moe": gain_moe, "w_query": w_query, "w_key": w_key, "w_value": w_value, "w_attn_out": w_attn_out, "w_router": w_router, "rel_bias": rel_bias, "w_in": w_in, "w_out": w_out, "cotangent": cotangent}


@jax.custom_vjp
def low(v):
    return lax.optimization_barrier(v.astype(jnp.bfloat16)).astype(jnp.float32)

@jax.custom_vjp
def low_back(v):
    return v

def low_keep(v):
    return (low(v), None)

def low_pass(kept, grad):
    return (grad,)

def back_keep(v):
    return (v, None)

def back_low(kept, grad):
    return (low(grad),)
low.defvjp(low_keep, low_pass)
low_back.defvjp(back_keep, back_low)
EPS = 1e-06
NEG_FILL = -1e+30
HIGHEST = lax.Precision.HIGHEST

def matmul(left, right):
    return jnp.dot(left, right, precision=HIGHEST)

def rms_norm(operand, gain):
    return operand * lax.rsqrt(lax.optimization_barrier(jnp.mean(operand * operand, axis=-1, keepdims=True)) + EPS) * gain

def segment_ids(seq_lens, count):
    starts = (jnp.cumsum(seq_lens) - seq_lens).astype(jnp.int32)
    places = jnp.arange(count, dtype=jnp.int32)
    return (lax.optimization_barrier(jnp.sum((places[:, None] >= starts[None, :]).astype(jnp.int32), axis=1)) - 1).astype(jnp.int32)

def group_attention(queries, keys_in, values_in, segment, bias_all):
    raw = jnp.einsum('qhd,khd->hqk', queries, keys_in, precision=HIGHEST) * DH ** (-0.5) + bias_all
    same_seq = segment[:, None] == segment[None, :]
    scores = low_back(jnp.where(same_seq[None], raw, NEG_FILL))
    weights_row = low(jax.nn.softmax(scores, axis=-1))
    return jnp.einsum('hqk,khd->qhd', weights_row, values_in, precision=HIGHEST)

def expert_apply(bundle):
    rows_in, weight_in, weight_out = bundle
    hidden = low_back(matmul(rows_in, weight_in))
    activated = low(jax.nn.gelu(hidden, approximate=False))
    return matmul(activated, weight_out)

def reference(layer_input, seq_lengths, expert_ids, bucket_table, gain_attn, gain_moe, w_query, w_key, w_value, w_attn_out, w_router, rel_bias, w_in, w_out, cotangent):
    groups = seq_lengths.shape[0]
    segments = jax.vmap(lambda row: segment_ids(row, TOK_GRP))(seq_lengths)
    places = jnp.arange(TOK_GRP, dtype=jnp.int32)
    rel_index = jnp.clip(places[None, :] - places[:, None] + MAXLEN - 1, 0, 2 * MAXLEN - 2).astype(jnp.int32)
    bucket = bucket_table[rel_index]
    expert_row = expert_ids[:, 0].reshape(groups, TOK_GRP).astype(jnp.int32)
    one_hot = (expert_row[..., None] == jnp.arange(EXPERTS, dtype=jnp.int32)).astype(jnp.int32)
    slot_index = lax.optimization_barrier(jnp.sum((jnp.cumsum(one_hot, axis=1).astype(jnp.int32) - one_hot) * one_hot, axis=-1)).astype(jnp.int32)
    group_base = (jnp.arange(groups, dtype=jnp.int32) * CAP)[:, None]
    destination = (expert_row * (groups * CAP) + group_base + slot_index).reshape(-1).astype(jnp.int32)
    choose = one_hot.reshape(-1, EXPERTS).astype(jnp.float32)

    def forward(input_f, gain_one, gain_two, query_w, key_w, value_w, out_w, router_w, bias_w, inner_w, outer_w):
        xn1 = low(rms_norm(input_f, gain_one))
        queries = low_back(low(matmul(xn1, query_w))).reshape(groups, TOK_GRP, H, DH)
        keys_all = low_back(low(matmul(xn1, key_w))).reshape(groups, TOK_GRP, H, DH)
        values_all = low_back(low(matmul(xn1, value_w))).reshape(groups, TOK_GRP, H, DH)
        bias_all = jnp.transpose(bias_w[bucket], (2, 0, 1))
        head_out = lax.map(jax.checkpoint(lambda bundle: group_attention(bundle[0], bundle[1], bundle[2], bundle[3], bias_all)), (queries, keys_all, values_all, segments))
        head_out = low_back(low(head_out.reshape(-1, H * DH)))
        mixed = input_f + low_back(matmul(head_out, out_w))
        xn2 = low(rms_norm(mixed, gain_two))
        logits = low_back(matmul(xn2, router_w))
        gate_prob = lax.optimization_barrier(jnp.sum(jax.nn.softmax(logits, axis=-1) * choose, axis=-1))
        buffer = jnp.zeros((EXPERTS * groups * CAP, D), jnp.float32).at[destination].set(xn2)
        buffer = buffer.reshape(EXPERTS, groups * CAP, D)
        partial_value = lax.map(jax.checkpoint(expert_apply), (buffer, inner_w, outer_w))
        expert_y = low_back(low(partial_value.reshape(-1, D)))[destination]
        return mixed + gate_prob[:, None] * expert_y
    floats = (layer_input.astype(jnp.float32), gain_attn.astype(jnp.float32), gain_moe.astype(jnp.float32), w_query.astype(jnp.float32), w_key.astype(jnp.float32), w_value.astype(jnp.float32), w_attn_out.astype(jnp.float32), w_router.astype(jnp.float32), rel_bias.astype(jnp.float32), w_in.astype(jnp.float32), w_out.astype(jnp.float32))
    result, pullback = jax.vjp(forward, *floats)
    grads = pullback(cotangent.astype(jnp.float32))
    return (result.astype(jnp.bfloat16), grads[0], grads[1], grads[2], grads[3], grads[4], grads[5], grads[6], grads[7], grads[8], grads[9], grads[10])
```

```python
import jax
import jax.numpy as jnp
from jax import lax
from jax.experimental import pallas as pl
from jax.experimental.pallas import tpu as pltpu
from jax.sharding import PartitionSpec as P

DH = 64
EPS = 1e-06
NEG_FILL = -1e30
MESH = pl.DeviceIdType.MESH
VMEM_BYTES = 44 * 1024 * 1024


def round_up(count, unit):
    return (count + unit - 1) // unit * unit


def contract_rows(left, right):
    return lax.dot_general(
        left, right, (((0,), (0,)), ((), ())), preferred_element_type=jnp.float32
    )


def contract_cols(left, right):
    return lax.dot_general(
        left, right, (((1,), (1,)), ((), ())), preferred_element_type=jnp.float32
    )


def matmul(left, right):
    return jnp.dot(left, right, preferred_element_type=jnp.float32)


def norm_back(grad_norm, unit_rows, inv_rms, gain):
    scaled = grad_norm * gain
    return inv_rms * (scaled - unit_rows * jnp.mean(scaled * unit_rows, axis=-1, keepdims=True))


def greet(axes):
    barrier = pltpu.get_barrier_semaphore()
    total = 0
    for axis in axes:
        size = lax.axis_size(axis)
        me = lax.axis_index(axis)
        for shift in range(1, size):
            pl.semaphore_signal(
                barrier,
                inc=1,
                device_id={axis: lax.rem(me + shift, size)},
                device_id_type=MESH,
            )
        total += size - 1
    pl.semaphore_wait(barrier, total)


def push(source, target, sems, slot, axis, peer):
    copy = pltpu.make_async_remote_copy(
        src_ref=source,
        dst_ref=target,
        send_sem=sems.at[(0,) + slot],
        recv_sem=sems.at[(1,) + slot],
        device_id={axis: peer},
        device_id_type=MESH,
    )
    copy.start()
    return copy


def sibling_of(place):
    return place + 1 - 2 * lax.rem(place, 2)


class Swap:
    def __init__(self, axis):
        self.axis = axis

    def sems(self):
        return pltpu.SemaphoreType.DMA((2, lax.axis_size(self.axis)))

    def start(self, source, target, sems):
        size = lax.axis_size(self.axis)
        me = lax.axis_index(self.axis)
        self.copies = []
        for shift in range(1, size):
            peer = lax.rem(me + shift, size)
            self.copies.append(
                push(source.at[peer], target.at[me], sems, (shift,), self.axis, peer)
            )
        target[me] = source[me]

    def middle(self):
        pass

    def finish(self):
        for copy in self.copies:
            copy.wait()


class Gather:
    def __init__(self, axis):
        self.axis = axis

    def sems(self):
        return pltpu.SemaphoreType.DMA((2, 2, lax.axis_size(self.axis) // 2))

    def start(self, source, target, sems):
        size = lax.axis_size(self.axis)
        me = lax.axis_index(self.axis)
        self.target, self.s, self.size, self.me = target, sems, size, me
        self.copies = []
        for shift in range(1, size // 2):
            peer = lax.rem(me + 2 * shift, size)
            self.copies.append(push(source, target.at[me], sems, (0, shift), self.axis, peer))
        self.passed = [push(source, target.at[me], sems, (1, 0), self.axis, sibling_of(me))]
        target[me] = source[...]

    def middle(self):
        for shift in range(1, self.size // 2):
            self.copies[shift - 1].wait_recv()
            origin = lax.rem(self.me + self.size - 2 * shift, self.size)
            block = self.target.at[origin]
            self.passed.append(
                push(block, block, self.s, (1, shift), self.axis, sibling_of(self.me))
            )

    def finish(self):
        for copy in self.copies:
            copy.wait_send()
        for copy in self.passed:
            copy.wait()


def transfer(number, axes, moves, operands, shapes):
    count = len(moves)

    def kernel(*refs):
        sources, targets, sems = refs[:count], refs[count : 2 * count], refs[2 * count :]
        greet(axes)
        for move, source, target, sem in zip(moves, sources, targets, sems):
            move.start(source, target, sem)
        for move in moves:
            move.middle()
        for move in moves:
            move.finish()

    return pl.pallas_call(
        kernel,
        out_shape=[jax.ShapeDtypeStruct(s, o.dtype) for s, o in zip(shapes, operands)],
        in_specs=[pl.BlockSpec(memory_space=pltpu.VMEM)] * count,
        out_specs=[pl.BlockSpec(memory_space=pltpu.VMEM)] * count,
        scratch_shapes=[move.sems() for move in moves],
        compiler_params=pltpu.CompilerParams(
            collective_id=number, has_side_effects=True, vmem_limit_bytes=VMEM_BYTES
        ),
    )(*operands)


def swap_rows(number, operand):
    return transfer(number, ("tensor",), [Swap("tensor")], [operand], [operand.shape])[0]


def to_experts(number, operand):
    size, slots, columns = operand.shape
    ranks = lax.axis_size("tensor")

    def kernel(source, target, far, near):
        me, rank = lax.axis_index("dp"), lax.axis_index("tensor")
        across, beside = lax.rem(rank + 2, ranks), sibling_of(rank)
        greet(("dp", "tensor"))
        arrivals = [None]
        for shift in range(1, size):
            peer = lax.rem(me + shift, size)
            arrivals.append(push(source.at[peer], target.at[rank, me], far, (shift,), "dp", peer))
        target[rank, me] = source[me]
        first, second, third = [], [], []

        def relay(shift):
            first[shift].wait_recv()
            block = target.at[across, lax.rem(me + size - shift, size)]
            third.append(push(block, block, near, (2, shift), "tensor", beside))

        for shift in range(size):
            if shift > 0:
                arrivals[shift].wait_recv()
            block = target.at[rank, lax.rem(me + size - shift, size)]
            first.append(push(block, block, near, (0, shift), "tensor", across))
            second.append(push(block, block, near, (1, shift), "tensor", beside))
            if shift > 0:
                relay(shift - 1)
        relay(size - 1)
        for copy in arrivals[1:] + first:
            copy.wait_send()
        for copy in second + third:
            copy.wait()

    return pl.pallas_call(
        kernel,
        out_shape=jax.ShapeDtypeStruct((ranks, size, slots, columns), operand.dtype),
        in_specs=[pl.BlockSpec(memory_space=pltpu.VMEM)],
        out_specs=pl.BlockSpec(memory_space=pltpu.VMEM),
        scratch_shapes=[
            pltpu.SemaphoreType.DMA((2, size)),
            pltpu.SemaphoreType.DMA((2, 3, size)),
        ],
        compiler_params=pltpu.CompilerParams(
            collective_id=number, has_side_effects=True, vmem_limit_bytes=VMEM_BYTES
        ),
    )(operand)


def from_experts(number, operand):
    ranks, size, slots, columns = operand.shape

    def kernel(source, target, held, total, far, near):
        me, rank = lax.axis_index("dp"), lax.axis_index("tensor")
        greet(("dp", "tensor"))
        order = list(range(1, size)) + [0]
        pieces = {}
        for shift in order:
            group = lax.rem(me + shift, size)
            for step in range(1, ranks):
                peer = lax.rem(rank + step, ranks)
                pieces[shift, step] = push(
                    source.at[peer, group],
                    held.at[step, group],
                    near,
                    (step, shift),
                    "tensor",
                    peer,
                )
        sent = []
        for shift in order:
            group = lax.rem(me + shift, size)
            summed = source[rank, group].astype(jnp.float32)
            for step in range(1, ranks):
                pieces[shift, step].wait_recv()
                summed = summed + held[step, group].astype(jnp.float32)
            if shift == 0:
                target[me] = summed.astype(operand.dtype)
            else:
                total[group] = summed.astype(operand.dtype)
                sent.append(push(total.at[group], target.at[me], far, (shift,), "dp", group))
        for copy in pieces.values():
            copy.wait_send()
        for copy in sent:
            copy.wait()

    return pl.pallas_call(
        kernel,
        out_shape=jax.ShapeDtypeStruct((size, slots, columns), operand.dtype),
        in_specs=[pl.BlockSpec(memory_space=pltpu.VMEM)],
        out_specs=pl.BlockSpec(memory_space=pltpu.VMEM),
        scratch_shapes=[
            pltpu.VMEM((ranks, size, slots, columns), operand.dtype),
            pltpu.VMEM((size, slots, columns), operand.dtype),
            pltpu.SemaphoreType.DMA((2, size)),
            pltpu.SemaphoreType.DMA((2, ranks, size)),
        ],
        compiler_params=pltpu.CompilerParams(
            collective_id=number, has_side_effects=True, vmem_limit_bytes=VMEM_BYTES
        ),
    )(operand)


def last_sums(number, rows, weights, small):
    size, ranks = lax.axis_size("dp"), lax.axis_size("tensor")
    swap_t, swap_d = Swap("tensor"), Swap("dp")
    gather_t, gather_d = Gather("tensor"), Gather("dp")

    def kernel(rows_in, weights_in, small_in, rows_out, weights_out, small_out, held, total, *sems):
        greet(("dp", "tensor"))
        gather_t.start(small_in, held, sems[0])
        swap_d.start(weights_in, weights_out, sems[1])
        swap_t.start(rows_in, rows_out, sems[2])
        gather_t.middle()
        gather_t.finish()
        summed = held[0]
        for rank in range(1, ranks):
            summed = summed + held[rank]
        total[...] = summed
        gather_d.start(total, small_out, sems[3])
        swap_t.finish()
        swap_d.finish()
        gather_d.middle()
        gather_d.finish()

    return pl.pallas_call(
        kernel,
        out_shape=[
            jax.ShapeDtypeStruct(rows.shape, rows.dtype),
            jax.ShapeDtypeStruct(weights.shape, weights.dtype),
            jax.ShapeDtypeStruct((size,) + small.shape, small.dtype),
        ],
        in_specs=[pl.BlockSpec(memory_space=pltpu.VMEM)] * 3,
        out_specs=[pl.BlockSpec(memory_space=pltpu.VMEM)] * 3,
        scratch_shapes=[
            pltpu.VMEM((ranks,) + small.shape, small.dtype),
            pltpu.VMEM(small.shape, small.dtype),
            gather_t.sems(),
            swap_d.sems(),
            swap_t.sems(),
            gather_d.sems(),
        ],
        compiler_params=pltpu.CompilerParams(
            collective_id=number, has_side_effects=True, vmem_limit_bytes=VMEM_BYTES
        ),
    )(rows, weights, small)


def head_probs(queries, keys, line, seg_rows, seg_cols):
    tokens = queries.shape[0]
    spread = jnp.broadcast_to(line, (tokens, 2 * tokens))
    bias = pltpu.roll(spread, 0, 1, stride=1, stride_axis=0)[:, :tokens]
    raw = contract_cols(queries, keys) * DH ** (-0.5) + bias
    scores = jnp.where(seg_rows == seg_cols, raw, NEG_FILL)
    expo = jnp.exp(scores - jnp.max(scores, axis=-1, keepdims=True))
    return expo / jnp.sum(expo, axis=-1, keepdims=True)


def attend(qkv, lines, seg_rows, seg_cols):
    tokens, heads = qkv.shape[0], lines.shape[0]
    width = heads * DH

    def kernel(qkv_ref, lines_ref, rows_ref, cols_ref, out_ref):
        parts = []
        for head in range(heads):
            lo = head * DH
            queries = qkv_ref[:, lo : lo + DH]
            keys = qkv_ref[:, width + lo : width + lo + DH]
            values = qkv_ref[:, 2 * width + lo : 2 * width + lo + DH]
            probs = head_probs(
                queries, keys, lines_ref[head : head + 1, :], rows_ref[...], cols_ref[...]
            )
            parts.append(matmul(probs.astype(jnp.bfloat16), values).astype(jnp.bfloat16))
        out_ref[...] = jnp.concatenate(parts, axis=1)

    return pl.pallas_call(
        kernel,
        out_shape=jax.ShapeDtypeStruct((tokens, width), jnp.bfloat16),
        in_specs=[pl.BlockSpec(memory_space=pltpu.VMEM)] * 4,
        out_specs=pl.BlockSpec(memory_space=pltpu.VMEM),
        compiler_params=pltpu.CompilerParams(vmem_limit_bytes=VMEM_BYTES),
    )(qkv, lines, seg_rows, seg_cols)


def attend_back(qkv, lines, seg_rows, seg_cols, grad_heads):
    tokens, heads = qkv.shape[0], lines.shape[0]
    width = heads * DH

    def kernel(qkv_ref, lines_ref, rows_ref, cols_ref, grad_ref, out_ref, sums_ref):
        row = lax.broadcasted_iota(jnp.int32, (tokens, tokens), 0)
        col = lax.broadcasted_iota(jnp.int32, (tokens, tokens), 1)
        flip = (row + col == tokens - 1).astype(jnp.float32).astype(jnp.bfloat16)
        grads_q, grads_k, grads_v = [], [], []
        for head in range(heads):
            lo = head * DH
            queries = qkv_ref[:, lo : lo + DH]
            keys = qkv_ref[:, width + lo : width + lo + DH]
            values = qkv_ref[:, 2 * width + lo : 2 * width + lo + DH]
            grad = grad_ref[:, lo : lo + DH]
            probs = head_probs(
                queries, keys, lines_ref[head : head + 1, :], rows_ref[...], cols_ref[...]
            )
            grads_v.append(contract_rows(probs.astype(jnp.bfloat16), grad))
            grad_probs = contract_cols(grad, values)
            mean = jnp.sum(probs * grad_probs, axis=-1, keepdims=True)
            grad_scores = (probs * (grad_probs - mean)).astype(jnp.bfloat16)
            grads_q.append(matmul(grad_scores, keys) * DH ** (-0.5))
            grads_k.append(contract_rows(grad_scores, queries) * DH ** (-0.5))
            flipped = matmul(flip, grad_scores)
            padded = jnp.concatenate([flipped, jnp.zeros_like(flipped)], axis=1)
            lined = pltpu.roll(padded, 0, 1, stride=1, stride_axis=0)
            sums_ref[head : head + 1, :] = jnp.sum(lined, axis=0, keepdims=True)
        out_ref[...] = jnp.concatenate(grads_q + grads_k + grads_v, axis=1).astype(jnp.bfloat16)

    return pl.pallas_call(
        kernel,
        out_shape=[
            jax.ShapeDtypeStruct((tokens, 3 * width), jnp.bfloat16),
            jax.ShapeDtypeStruct((heads, 2 * tokens), jnp.float32),
        ],
        in_specs=[pl.BlockSpec(memory_space=pltpu.VMEM)] * 5,
        out_specs=[pl.BlockSpec(memory_space=pltpu.VMEM)] * 2,
        compiler_params=pltpu.CompilerParams(vmem_limit_bytes=VMEM_BYTES),
    )(qkv, lines, seg_rows, seg_cols, grad_heads)


def shards(
    layer_input,
    seq_lengths,
    expert_ids,
    bucket_table,
    gain_attn,
    gain_moe,
    w_query,
    w_key,
    w_value,
    w_attn_out,
    w_router,
    rel_bias,
    w_in,
    w_out,
    cotangent,
):
    float_type = jnp.float32
    half_type = jnp.bfloat16
    tok_dev, width = layer_input.shape
    group_tok = expert_ids.shape[0]
    experts = w_router.shape[1]
    groups, ranks = lax.axis_size("dp"), lax.axis_size("tensor")
    slots = round_up(group_tok // experts + 1, 16)
    local_heads = rel_bias.shape[1]
    head_cols = local_heads * DH
    max_length = (bucket_table.shape[0] + 1) // 2
    buckets = rel_bias.shape[0]
    row_dev = w_query.shape[0]
    row_pad = round_up(row_dev, 16)
    chunk = width // ranks
    tensor_rank = lax.axis_index("tensor")
    row_offset = tensor_rank * tok_dev

    places = jnp.arange(group_tok, dtype=jnp.int32)
    seq_lens = seq_lengths[0]
    seq_starts = jnp.cumsum(seq_lens) - seq_lens
    segment = jnp.sum((places[:, None] >= seq_starts[None, :]).astype(jnp.int32), axis=1) - 1
    seg_rows, seg_cols = segment[:, None], segment[None, :]
    line_bucket = jnp.concatenate(
        [
            bucket_table[max_length - 1 :],
            jnp.broadcast_to(bucket_table[-1:], (group_tok - max_length,)),
            jnp.broadcast_to(bucket_table[:1], (group_tok - max_length + 1,)),
            bucket_table[: max_length - 1],
        ]
    )
    line_hot = line_bucket[None, :] == jnp.arange(buckets, dtype=jnp.int32)[:, None]
    lines = contract_rows(rel_bias, line_hot.astype(half_type))

    input_f = layer_input.astype(float_type)
    gain_one = gain_attn.astype(float_type)
    inv_one = lax.rsqrt(jnp.mean(input_f * input_f, axis=-1, keepdims=True) + EPS)
    unit_one = input_f * inv_one
    normed_one = (unit_one * gain_one).astype(half_type)
    packed = jnp.concatenate([w_query, w_key, w_value, w_attn_out.T], axis=1)
    packed = jnp.pad(packed, ((0, row_pad - row_dev), (0, 0)))
    pack_cols = packed.shape[1]
    router_rows = round_up(experts, 16)
    router_cols = round_up(row_dev, 128)
    router_part = jnp.pad(
        w_router.T, ((0, router_rows - experts), (0, router_cols - row_dev))
    )
    packed_all, router_all, full_one = transfer(
        0,
        ("dp", "tensor"),
        [Gather("dp"), Gather("dp"), Gather("tensor")],
        [packed, router_part, normed_one],
        [
            (groups, row_pad, pack_cols),
            (groups, router_rows, router_cols),
            (ranks, tok_dev, width),
        ],
    )
    packed_all = packed_all[:, :row_dev].reshape(width, pack_cols)
    qkv_all, out_all = packed_all[:, : 3 * head_cols], packed_all[:, 3 * head_cols :]
    router_all = jnp.transpose(router_all[:, :experts, :row_dev], (1, 0, 2)).reshape(
        experts, width
    )
    full_one = full_one.reshape(group_tok, width)

    qkv = matmul(full_one, qkv_all).astype(half_type)
    head_out = attend(qkv, lines, seg_rows, seg_cols)
    attn_part = contract_cols(head_out, out_all).astype(half_type)
    attn_parts = swap_rows(1, attn_part.reshape(ranks, tok_dev, width))
    mixed = input_f + jnp.sum(attn_parts.astype(float_type), axis=0)

    gain_two = gain_moe.astype(float_type)
    inv_two = lax.rsqrt(jnp.mean(mixed * mixed, axis=-1, keepdims=True) + EPS)
    unit_two = mixed * inv_two
    normed_two = (unit_two * gain_two).astype(half_type)
    logits = contract_cols(normed_two, router_all)
    router_prob = jax.nn.softmax(logits, axis=-1)
    expert_row = expert_ids[:, 0]
    one_hot = (expert_row[:, None] == jnp.arange(experts, dtype=jnp.int32)[None, :]).astype(
        jnp.int32
    )
    earlier = (places[:, None] > places[None, :]).astype(half_type)
    before = matmul(earlier, one_hot.astype(half_type)).astype(jnp.int32)
    slot_index = jnp.sum(before * one_hot, axis=1)
    destination = expert_row * slots + slot_index
    place_hot = (
        destination[:, None] == jnp.arange(experts * slots, dtype=jnp.int32)[None, :]
    ).astype(half_type)
    own_choice = lax.dynamic_slice_in_dim(one_hot, row_offset, tok_dev, 0).astype(float_type)
    gate_prob = jnp.sum(router_prob * own_choice, axis=1, keepdims=True)
    grad_out = cotangent.astype(float_type)
    grad_y = (gate_prob * grad_out).astype(half_type)

    both = jnp.concatenate(
        [normed_two.reshape(tok_dev, ranks, chunk), grad_y.reshape(tok_dev, ranks, chunk)], axis=2
    )
    both = swap_rows(2, jnp.transpose(both, (1, 0, 2))).reshape(group_tok, 2 * chunk)
    buffer = contract_rows(place_hot, both).astype(half_type)
    arrived = to_experts(3, buffer.reshape(experts, slots, 2 * chunk))
    arrived = jnp.transpose(arrived.reshape(ranks, groups * slots, 2, chunk), (2, 1, 0, 3))
    arrived = arrived.reshape(2, groups * slots, width)
    rows, grad_rows_y = arrived[0], arrived[1]

    hidden = matmul(rows, w_in[0])
    activated = jax.nn.gelu(hidden, approximate=False).astype(half_type)
    partial_value = matmul(activated, w_out[0])
    grad_w_out = contract_rows(activated, grad_rows_y)
    grad_act = contract_cols(grad_rows_y, w_out[0])
    grad_hidden = jax.vjp(lambda operand: jax.nn.gelu(operand, approximate=False), hidden)[1](
        grad_act
    )[0].astype(half_type)
    grad_w_in = contract_rows(rows, grad_hidden)
    grad_rows = contract_cols(grad_hidden, w_in[0])

    back = jnp.concatenate(
        [
            partial_value.astype(half_type).reshape(groups * slots, ranks, chunk),
            grad_rows.astype(half_type).reshape(groups * slots, ranks, chunk),
        ],
        axis=2,
    )
    back = jnp.transpose(back, (1, 0, 2)).reshape(ranks, groups, slots, 2 * chunk)
    returned = from_experts(4, back).reshape(experts * slots, 2 * chunk)
    returned = matmul(place_hot, returned).astype(half_type)
    returned = swap_rows(5, returned.reshape(ranks, tok_dev, 2 * chunk))
    returned = jnp.transpose(returned.reshape(ranks, tok_dev, 2, chunk), (2, 1, 0, 3))
    returned = returned.reshape(2, tok_dev, width).astype(float_type)
    expert_y, grad_norm_two = returned[0], returned[1]
    layer_output = (mixed + gate_prob * expert_y).astype(half_type)
    grad_gate = jnp.sum(grad_out * expert_y, axis=1, keepdims=True)
    grad_logits = (router_prob * (own_choice - gate_prob) * grad_gate).astype(half_type)
    grad_router = contract_rows(grad_logits, normed_two)
    grad_norm_two = grad_norm_two + matmul(grad_logits, router_all)
    gain_two_part = jnp.sum(grad_norm_two * unit_two, axis=0)
    grad_mixed = grad_out + norm_back(grad_norm_two, unit_two, inv_two, gain_two)

    grad_attn = transfer(
        6,
        ("tensor",),
        [Gather("tensor")],
        [grad_mixed.astype(half_type)],
        [(ranks, tok_dev, width)],
    )[0].reshape(group_tok, width)
    grad_out_proj = contract_rows(grad_attn, head_out)
    grad_heads = matmul(grad_attn, out_all).astype(half_type)
    grad_qkv, line_sums = attend_back(qkv, lines, seg_rows, seg_cols, grad_heads)
    sums_hot = jnp.roll(line_hot, group_tok - 1, axis=1).astype(float_type)
    grad_bucket = lax.dot_general(
        line_sums, sums_hot, (((1,), (1,)), ((), ())), precision=lax.Precision.HIGHEST
    )
    grad_full_one = contract_cols(grad_qkv, qkv_all)
    gain_one_part = jnp.sum(grad_full_one * full_one.astype(float_type), axis=0) / gain_one
    grad_weights = jnp.concatenate(
        [contract_rows(full_one, grad_qkv), grad_out_proj], axis=1
    ).astype(half_type)
    grad_weights = jnp.pad(
        grad_weights.reshape(groups, row_dev, pack_cols),
        ((0, 0), (0, row_pad - row_dev), (0, 0)),
    )
    bias_flat = grad_bucket.reshape(1, local_heads * buckets)
    bias_row = jnp.pad(bias_flat, ((0, 0), (0, width - local_heads * buckets)))
    own_rank = (jnp.arange(ranks, dtype=jnp.int32) == tensor_rank).astype(float_type)
    small = jnp.concatenate(
        [gain_one_part[None], gain_two_part[None], own_rank[:, None] * bias_row, grad_router]
    )
    small = jnp.pad(small, ((0, round_up(small.shape[0], 8) - small.shape[0]), (0, 0)))
    norm_parts, weight_parts, small_parts = last_sums(
        7, grad_full_one.astype(half_type).reshape(ranks, tok_dev, width), grad_weights, small
    )
    grad_norm_one = jnp.sum(norm_parts.astype(float_type), axis=0)
    grad_input = grad_mixed + norm_back(grad_norm_one, unit_one, inv_one, gain_one)
    weight_sums = jnp.sum(weight_parts[:, :row_dev].astype(float_type), axis=0)
    small_sums = jnp.sum(small_parts, axis=0)
    router_sum = lax.dynamic_slice(
        small_sums, (2 + ranks, lax.axis_index("dp") * row_dev), (experts, row_dev)
    )
    bias_sum = lax.dynamic_slice_in_dim(small_sums, 2 + tensor_rank, 1, 0)
    bias_sum = bias_sum[0, : local_heads * buckets].reshape(local_heads, buckets)
    return (
        layer_output,
        grad_input,
        small_sums[0],
        small_sums[1],
        weight_sums[:, :head_cols],
        weight_sums[:, head_cols : 2 * head_cols],
        weight_sums[:, 2 * head_cols : 3 * head_cols],
        weight_sums[:, 3 * head_cols :].T,
        router_sum.T,
        bias_sum.T,
        grad_w_in[None],
        grad_w_out[None],
    )


def solution(mesh):
    return jax.shard_map(
        shards,
        mesh=mesh,
        in_specs=(
            P(("dp", "tensor"), None),
            P("dp", None),
            P("dp", None),
            P(),
            P(),
            P(),
            P("dp", "tensor"),
            P("dp", "tensor"),
            P("dp", "tensor"),
            P("tensor", "dp"),
            P("dp", None),
            P(None, "tensor"),
            P("dp", None, "tensor"),
            P("dp", "tensor", None),
            P(("dp", "tensor"), None),
        ),
        out_specs=(
            P(("dp", "tensor"), None),
            P(("dp", "tensor"), None),
            P(),
            P(),
            P("dp", "tensor"),
            P("dp", "tensor"),
            P("dp", "tensor"),
            P("tensor", "dp"),
            P("dp", None),
            P(None, "tensor"),
            P("dp", None, "tensor"),
            P("dp", "tensor", None),
        ),
        check_vma=False,
    )
```

```python
import jax
import jax.numpy as jnp
from jax import lax
from jax.experimental import pallas as pl
from jax.experimental.pallas import tpu as pltpu
from jax.sharding import PartitionSpec as P

DH = 64
EPS = 1e-06
NEG_FILL = -1e30
MESH = pl.DeviceIdType.MESH
VMEM_BYTES = 44 * 1024 * 1024


def round_up(count, unit):
    return (count + unit - 1) // unit * unit


def contract_rows(left, right):
    return lax.dot_general(
        left, right, (((0,), (0,)), ((), ())), preferred_element_type=jnp.float32
    )


def contract_cols(left, right):
    return lax.dot_general(
        left, right, (((1,), (1,)), ((), ())), preferred_element_type=jnp.float32
    )


def matmul(left, right):
    return jnp.dot(left, right, preferred_element_type=jnp.float32)


def norm_back(grad_norm, unit_rows, inv_rms, gain):
    scaled = grad_norm * gain
    return inv_rms * (scaled - unit_rows * jnp.mean(scaled * unit_rows, axis=-1, keepdims=True))


def greet(axes):
    barrier = pltpu.get_barrier_semaphore()
    total = 0
    for axis in axes:
        size = lax.axis_size(axis)
        me = lax.axis_index(axis)
        for shift in range(1, size):
            pl.semaphore_signal(
                barrier,
                inc=1,
                device_id={axis: lax.rem(me + shift, size)},
                device_id_type=MESH,
            )
        total += size - 1
    pl.semaphore_wait(barrier, total)


def push(source, target, sems, slot, axis, peer):
    copy = pltpu.make_async_remote_copy(
        src_ref=source,
        dst_ref=target,
        send_sem=sems.at[(0,) + slot],
        recv_sem=sems.at[(1,) + slot],
        device_id={axis: peer},
        device_id_type=MESH,
    )
    copy.start()
    return copy


def sibling_of(place):
    return place + 1 - 2 * lax.rem(place, 2)


class Swap:
    def __init__(self, axis):
        self.axis = axis

    def sems(self):
        return pltpu.SemaphoreType.DMA((2, lax.axis_size(self.axis)))

    def start(self, source, target, sems):
        size = lax.axis_size(self.axis)
        me = lax.axis_index(self.axis)
        self.copies = []
        for shift in range(1, size):
            peer = lax.rem(me + shift, size)
            self.copies.append(
                push(source.at[peer], target.at[me], sems, (shift,), self.axis, peer)
            )
        target[me] = source[me]

    def middle(self):
        pass

    def finish(self):
        for copy in self.copies:
            copy.wait()


class Gather:
    def __init__(self, axis):
        self.axis = axis

    def sems(self):
        return pltpu.SemaphoreType.DMA((2, 2, lax.axis_size(self.axis) // 2))

    def start(self, source, target, sems):
        size = lax.axis_size(self.axis)
        me = lax.axis_index(self.axis)
        self.target, self.s, self.size, self.me = target, sems, size, me
        self.copies = []
        for shift in range(1, size // 2):
            peer = lax.rem(me + 2 * shift, size)
            self.copies.append(push(source, target.at[me], sems, (0, shift), self.axis, peer))
        self.passed = [push(source, target.at[me], sems, (1, 0), self.axis, sibling_of(me))]
        target[me] = source[...]

    def middle(self):
        for shift in range(1, self.size // 2):
            self.copies[shift - 1].wait_recv()
            origin = lax.rem(self.me + self.size - 2 * shift, self.size)
            block = self.target.at[origin]
            self.passed.append(
                push(block, block, self.s, (1, shift), self.axis, sibling_of(self.me))
            )

    def finish(self):
        for copy in self.copies:
            copy.wait_send()
        for copy in self.passed:
            copy.wait()


class Reduce:
    def __init__(self, axis, shape, dtype):
        self.axis = axis
        self.half = lax.axis_size(axis) // 2
        self.block, self.dtype = tuple(shape), dtype

    def scratch(self):
        slots = pltpu.VMEM((3, self.half) + self.block, self.dtype)
        return [slots, pltpu.SemaphoreType.DMA((2, 2, self.half))]

    def start(self, source, slots, sems):
        self.source, self.slots, self.s = source, slots, sems
        self.size, self.me = lax.axis_size(self.axis), lax.axis_index(self.axis)
        sibling = sibling_of(self.me)
        self.near = {}
        for shift in list(range(1, self.half)) + [0]:
            block = source.at[lax.rem(sibling + 2 * shift, self.size)]
            self.near[shift] = push(
                block, slots.at[0, shift], sems, (0, shift), self.axis, sibling
            )

    def middle(self):
        self.far = {}
        for shift in range(1, self.half):
            self.near[shift].wait_recv()
            peer = lax.rem(self.me + 2 * shift, self.size)
            pair = self.source[peer].astype(jnp.float32)
            pair = pair + self.slots[0, shift].astype(jnp.float32)
            self.slots[1, shift] = pair.astype(self.dtype)
            self.far[shift] = push(
                self.slots.at[1, shift],
                self.slots.at[2, shift],
                self.s,
                (1, shift),
                self.axis,
                peer,
            )

    def finish(self, target):
        self.near[0].wait_recv()
        summed = self.source[self.me].astype(jnp.float32)
        summed = summed + self.slots[0, 0].astype(jnp.float32)
        for shift in range(1, self.half):
            self.far[shift].wait_recv()
            summed = summed + self.slots[2, shift].astype(jnp.float32)
        target[...] = summed
        for copy in list(self.near.values()) + list(self.far.values()):
            copy.wait_send()


def sum_rows(number, operand):
    move = Reduce("tensor", operand.shape[1:], operand.dtype)

    def kernel(source, target, slots, sems):
        greet(("tensor",))
        move.start(source, slots, sems)
        move.middle()
        move.finish(target)

    return pl.pallas_call(
        kernel,
        out_shape=jax.ShapeDtypeStruct(operand.shape[1:], jnp.float32),
        in_specs=[pl.BlockSpec(memory_space=pltpu.VMEM)],
        out_specs=pl.BlockSpec(memory_space=pltpu.VMEM),
        scratch_shapes=move.scratch(),
        compiler_params=pltpu.CompilerParams(
            collective_id=number, has_side_effects=True, vmem_limit_bytes=VMEM_BYTES
        ),
    )(operand)


def transfer(number, axes, moves, operands, shapes):
    count = len(moves)

    def kernel(*refs):
        sources, targets, sems = refs[:count], refs[count : 2 * count], refs[2 * count :]
        greet(axes)
        for move, source, target, sem in zip(moves, sources, targets, sems):
            move.start(source, target, sem)
        for move in moves:
            move.middle()
        for move in moves:
            move.finish()

    return pl.pallas_call(
        kernel,
        out_shape=[jax.ShapeDtypeStruct(s, o.dtype) for s, o in zip(shapes, operands)],
        in_specs=[pl.BlockSpec(memory_space=pltpu.VMEM)] * count,
        out_specs=[pl.BlockSpec(memory_space=pltpu.VMEM)] * count,
        scratch_shapes=[move.sems() for move in moves],
        compiler_params=pltpu.CompilerParams(
            collective_id=number, has_side_effects=True, vmem_limit_bytes=VMEM_BYTES
        ),
    )(*operands)


def swap_rows(number, operand):
    return transfer(number, ("tensor",), [Swap("tensor")], [operand], [operand.shape])[0]


def visit_experts(number, operand, weight_in, weight_out):
    size, slots, columns = operand.shape
    ranks = lax.axis_size("tensor")
    chunk = columns // 2
    width, units = weight_in.shape
    half_type, float_type = jnp.bfloat16, jnp.float32
    steps = min(4, size)
    share = size // steps
    step_rows = share * slots

    def kernel(
        source, w_in, w_out, target, grad_in, grad_out,
        arrived, back, held, pairs, got, total, rows, grads, acts, hids, far, near, home, ret,
    ):
        me, rank = lax.axis_index("dp"), lax.axis_index("tensor")
        across, beside = lax.rem(rank + 2, ranks), sibling_of(rank)
        aslant = lax.rem(beside + 2, ranks)
        groups = [lax.rem(me + size - shift, size) for shift in range(size)]
        greet(("dp", "tensor"))
        arrivals = [None]
        for shift in range(1, size):
            peer = lax.rem(me + shift, size)
            arrivals.append(push(source.at[peer], arrived.at[rank, me], far, (shift,), "dp", peer))
        arrived[rank, me] = source[me]
        first, second, third = {}, {}, {}
        kept, passed, crossed, sent = {}, {}, {}, {}

        def spread(step):
            for shift in range(step * share, (step + 1) * share):
                if shift > 0:
                    arrivals[shift].wait_recv()
                block = arrived.at[rank, groups[shift]]
                first[shift] = push(block, block, near, (0, shift), "tensor", across)
                second[shift] = push(block, block, near, (1, shift), "tensor", beside)

        def relay(step):
            for shift in range(step * share, (step + 1) * share):
                first[shift].wait_recv()
                block = arrived.at[across, groups[shift]]
                third[shift] = push(block, block, near, (2, shift), "tensor", beside)

        def compute(step):
            lo = step * step_rows
            for place in range(share):
                shift = step * share + place
                second[shift].wait_recv()
                third[shift].wait_recv()
                blocks = [arrived[place_t, groups[shift]] for place_t in range(ranks)]
                at = slice(lo + place * slots, lo + (place + 1) * slots)
                rows[at, :] = jnp.concatenate([block[:, :chunk] for block in blocks], axis=1)
                grads[at, :] = jnp.concatenate([block[:, chunk:] for block in blocks], axis=1)
            part = slice(lo, lo + step_rows)
            hidden = matmul(rows[part, :], w_in[...])
            below = 0.5 + 0.5 * lax.erf(hidden * (0.5**0.5))
            slope = below + hidden * jnp.exp(-0.5 * hidden * hidden) * 0.3989422804014327
            activated = (hidden * below).astype(half_type)
            acts[part, :] = activated
            grad_act = contract_cols(grads[part, :], w_out[...])
            grad_hidden = (grad_act * slope).astype(half_type)
            hids[part, :] = grad_hidden
            value = matmul(activated, w_out[...]).astype(half_type)
            grad_rows = contract_cols(grad_hidden, w_in[...]).astype(half_type)
            for place in range(share):
                shift = step * share + place
                at = slice(place * slots, (place + 1) * slots)
                for place_t in range(ranks):
                    cols = slice(place_t * chunk, (place_t + 1) * chunk)
                    back[place_t, groups[shift]] = jnp.concatenate(
                        [value[at, cols], grad_rows[at, cols]], axis=1
                    )

        def pair_up(step):
            for shift in range(step * share, (step + 1) * share):
                group = groups[shift]
                passed[shift] = push(
                    back.at[aslant, group], held.at[1, group], home, (1, shift), "tensor", beside
                )
                kept[shift] = push(
                    back.at[beside, group], held.at[0, group], home, (0, shift), "tensor", beside
                )

        def cross(step):
            for shift in range(step * share, (step + 1) * share):
                group = groups[shift]
                passed[shift].wait_recv()
                pair = back[across, group].astype(float_type) + held[1, group].astype(float_type)
                pairs[group] = pair.astype(half_type)
                crossed[shift] = push(
                    pairs.at[group], got.at[group], home, (2, shift), "tensor", across
                )

        def send_home(step):
            for shift in range(step * share, (step + 1) * share):
                group = groups[shift]
                kept[shift].wait_recv()
                crossed[shift].wait_recv()
                summed = back[rank, group].astype(float_type) + held[0, group].astype(float_type)
                summed = (summed + got[group].astype(float_type)).astype(half_type)
                if shift == 0:
                    target[me] = summed
                else:
                    total[group] = summed
                    sent[shift] = push(
                        total.at[group], target.at[me], ret, (shift,), "dp", group
                    )

        spread(0)
        for step in range(steps):
            relay(step)
            if step + 1 < steps:
                spread(step + 1)
            compute(step)
            pair_up(step)
            if step >= 1:
                cross(step - 1)
            if step >= 2:
                send_home(step - 2)
        if steps >= 2:
            send_home(steps - 2)
        cross(steps - 1)
        grad_out[...] = contract_rows(acts[...], grads[...])
        send_home(steps - 1)
        grad_in[...] = contract_rows(rows[...], hids[...])
        for copy in arrivals[1:]:
            copy.wait_send()
        for copies in (first, second, third, kept, passed, crossed):
            for copy in copies.values():
                copy.wait_send()
        for copy in sent.values():
            copy.wait()

    blocks = (size, slots, columns)
    return pl.pallas_call(
        kernel,
        out_shape=[
            jax.ShapeDtypeStruct(blocks, operand.dtype),
            jax.ShapeDtypeStruct(weight_in.shape, float_type),
            jax.ShapeDtypeStruct(weight_out.shape, float_type),
        ],
        in_specs=[pl.BlockSpec(memory_space=pltpu.VMEM)] * 3,
        out_specs=[pl.BlockSpec(memory_space=pltpu.VMEM)] * 3,
        scratch_shapes=[
            pltpu.VMEM((ranks,) + blocks, half_type),
            pltpu.VMEM((ranks,) + blocks, half_type),
            pltpu.VMEM((2,) + blocks, half_type),
            pltpu.VMEM(blocks, half_type),
            pltpu.VMEM(blocks, half_type),
            pltpu.VMEM(blocks, half_type),
            pltpu.VMEM((size * slots, width), half_type),
            pltpu.VMEM((size * slots, width), half_type),
            pltpu.VMEM((size * slots, units), half_type),
            pltpu.VMEM((size * slots, units), half_type),
            pltpu.SemaphoreType.DMA((2, size)),
            pltpu.SemaphoreType.DMA((2, 3, size)),
            pltpu.SemaphoreType.DMA((2, 3, size)),
            pltpu.SemaphoreType.DMA((2, size)),
        ],
        compiler_params=pltpu.CompilerParams(
            collective_id=number, has_side_effects=True, vmem_limit_bytes=VMEM_BYTES
        ),
    )(operand, weight_in, weight_out)


def last_sums(number, rows, weights, small):
    size, ranks = lax.axis_size("dp"), lax.axis_size("tensor")
    sum_t = Reduce("tensor", rows.shape[1:], rows.dtype)
    sum_d = Reduce("dp", weights.shape[1:], weights.dtype)
    gather_t, gather_d = Gather("tensor"), Gather("dp")

    def kernel(
        rows_in, weights_in, small_in, rows_out, weights_out, small_out,
        held, total, slots_t, sems_t, slots_d, sems_d, sems_g, sems_h,
    ):
        greet(("dp", "tensor"))
        sum_d.start(weights_in, slots_d, sems_d)
        gather_t.start(small_in, held, sems_g)
        sum_t.start(rows_in, slots_t, sems_t)
        gather_t.middle()
        sum_t.middle()
        sum_d.middle()
        gather_t.finish()
        summed = held[0]
        for rank in range(1, ranks):
            summed = summed + held[rank]
        total[...] = summed
        gather_d.start(total, small_out, sems_h)
        sum_t.finish(rows_out)
        gather_d.middle()
        sum_d.finish(weights_out)
        gather_d.finish()

    return pl.pallas_call(
        kernel,
        out_shape=[
            jax.ShapeDtypeStruct(rows.shape[1:], jnp.float32),
            jax.ShapeDtypeStruct(weights.shape[1:], jnp.float32),
            jax.ShapeDtypeStruct((size,) + small.shape, small.dtype),
        ],
        in_specs=[pl.BlockSpec(memory_space=pltpu.VMEM)] * 3,
        out_specs=[pl.BlockSpec(memory_space=pltpu.VMEM)] * 3,
        scratch_shapes=[
            pltpu.VMEM((ranks,) + small.shape, small.dtype),
            pltpu.VMEM(small.shape, small.dtype),
        ]
        + sum_t.scratch()
        + sum_d.scratch()
        + [gather_t.sems(), gather_d.sems()],
        compiler_params=pltpu.CompilerParams(
            collective_id=number, has_side_effects=True, vmem_limit_bytes=VMEM_BYTES
        ),
    )(rows, weights, small)


def head_probs(queries, keys, line, seg_rows, seg_cols):
    tokens = queries.shape[0]
    spread = jnp.broadcast_to(line, (tokens, 2 * tokens))
    bias = pltpu.roll(spread, 0, 1, stride=1, stride_axis=0)[:, :tokens]
    raw = contract_cols(queries, keys) * DH ** (-0.5) + bias
    scores = jnp.where(seg_rows == seg_cols, raw, NEG_FILL)
    expo = jnp.exp(scores - jnp.max(scores, axis=-1, keepdims=True))
    return expo / jnp.sum(expo, axis=-1, keepdims=True)


def attend(qkv, lines, seg_rows, seg_cols):
    tokens, heads = qkv.shape[0], lines.shape[0]
    width = heads * DH

    def kernel(qkv_ref, lines_ref, rows_ref, cols_ref, out_ref):
        parts = []
        for head in range(heads):
            lo = head * DH
            queries = qkv_ref[:, lo : lo + DH]
            keys = qkv_ref[:, width + lo : width + lo + DH]
            values = qkv_ref[:, 2 * width + lo : 2 * width + lo + DH]
            probs = head_probs(
                queries, keys, lines_ref[head : head + 1, :], rows_ref[...], cols_ref[...]
            )
            parts.append(matmul(probs.astype(jnp.bfloat16), values).astype(jnp.bfloat16))
        out_ref[...] = jnp.concatenate(parts, axis=1)

    return pl.pallas_call(
        kernel,
        out_shape=jax.ShapeDtypeStruct((tokens, width), jnp.bfloat16),
        in_specs=[pl.BlockSpec(memory_space=pltpu.VMEM)] * 4,
        out_specs=pl.BlockSpec(memory_space=pltpu.VMEM),
        compiler_params=pltpu.CompilerParams(vmem_limit_bytes=VMEM_BYTES),
    )(qkv, lines, seg_rows, seg_cols)


def attend_back(qkv, lines, seg_rows, seg_cols, grad_heads):
    tokens, heads = qkv.shape[0], lines.shape[0]
    width = heads * DH

    def kernel(qkv_ref, lines_ref, rows_ref, cols_ref, grad_ref, out_ref, sums_ref):
        row = lax.broadcasted_iota(jnp.int32, (tokens, tokens), 0)
        col = lax.broadcasted_iota(jnp.int32, (tokens, tokens), 1)
        flip = (row + col == tokens - 1).astype(jnp.float32).astype(jnp.bfloat16)
        grads_q, grads_k, grads_v = [], [], []
        for head in range(heads):
            lo = head * DH
            queries = qkv_ref[:, lo : lo + DH]
            keys = qkv_ref[:, width + lo : width + lo + DH]
            values = qkv_ref[:, 2 * width + lo : 2 * width + lo + DH]
            grad = grad_ref[:, lo : lo + DH]
            probs = head_probs(
                queries, keys, lines_ref[head : head + 1, :], rows_ref[...], cols_ref[...]
            )
            grads_v.append(contract_rows(probs.astype(jnp.bfloat16), grad))
            grad_probs = contract_cols(grad, values)
            mean = jnp.sum(probs * grad_probs, axis=-1, keepdims=True)
            grad_scores = (probs * (grad_probs - mean)).astype(jnp.bfloat16)
            grads_q.append(matmul(grad_scores, keys) * DH ** (-0.5))
            grads_k.append(contract_rows(grad_scores, queries) * DH ** (-0.5))
            flipped = matmul(flip, grad_scores)
            padded = jnp.concatenate([flipped, jnp.zeros_like(flipped)], axis=1)
            lined = pltpu.roll(padded, 0, 1, stride=1, stride_axis=0)
            sums_ref[head : head + 1, :] = jnp.sum(lined, axis=0, keepdims=True)
        out_ref[...] = jnp.concatenate(grads_q + grads_k + grads_v, axis=1).astype(jnp.bfloat16)

    return pl.pallas_call(
        kernel,
        out_shape=[
            jax.ShapeDtypeStruct((tokens, 3 * width), jnp.bfloat16),
            jax.ShapeDtypeStruct((heads, 2 * tokens), jnp.float32),
        ],
        in_specs=[pl.BlockSpec(memory_space=pltpu.VMEM)] * 5,
        out_specs=[pl.BlockSpec(memory_space=pltpu.VMEM)] * 2,
        compiler_params=pltpu.CompilerParams(vmem_limit_bytes=VMEM_BYTES),
    )(qkv, lines, seg_rows, seg_cols, grad_heads)


def shards(
    layer_input,
    seq_lengths,
    expert_ids,
    bucket_table,
    gain_attn,
    gain_moe,
    w_query,
    w_key,
    w_value,
    w_attn_out,
    w_router,
    rel_bias,
    w_in,
    w_out,
    cotangent,
):
    float_type = jnp.float32
    half_type = jnp.bfloat16
    tok_dev, width = layer_input.shape
    group_tok = expert_ids.shape[0]
    experts = w_router.shape[1]
    groups, ranks = lax.axis_size("dp"), lax.axis_size("tensor")
    slots = round_up(group_tok // experts + 1, 16)
    local_heads = rel_bias.shape[1]
    head_cols = local_heads * DH
    max_length = (bucket_table.shape[0] + 1) // 2
    buckets = rel_bias.shape[0]
    row_dev = w_query.shape[0]
    row_pad = round_up(row_dev, 16)
    chunk = width // ranks
    tensor_rank = lax.axis_index("tensor")
    row_offset = tensor_rank * tok_dev

    places = jnp.arange(group_tok, dtype=jnp.int32)
    segment = jnp.zeros_like(places)
    start = jnp.zeros((), jnp.int32)
    for sequence in range(seq_lengths.shape[1] - 1):
        start = start + seq_lengths[0, sequence]
        segment = segment + (places >= start).astype(jnp.int32)
    seg_rows, seg_cols = segment[:, None], segment[None, :]
    line_bucket = jnp.concatenate(
        [
            bucket_table[max_length - 1 :],
            jnp.broadcast_to(bucket_table[-1:], (group_tok - max_length,)),
            jnp.broadcast_to(bucket_table[:1], (group_tok - max_length + 1,)),
            bucket_table[: max_length - 1],
        ]
    )
    line_hot = line_bucket[None, :] == jnp.arange(buckets, dtype=jnp.int32)[:, None]
    lines = contract_rows(rel_bias, line_hot.astype(half_type))

    input_f = layer_input.astype(float_type)
    gain_one = gain_attn.astype(float_type)
    inv_one = lax.rsqrt(jnp.mean(input_f * input_f, axis=-1, keepdims=True) + EPS)
    unit_one = input_f * inv_one
    normed_one = (unit_one * gain_one).astype(half_type)
    packed = jnp.concatenate([w_query, w_key, w_value, w_attn_out.T], axis=1)
    packed = jnp.pad(packed, ((0, row_pad - row_dev), (0, 0)))
    pack_cols = packed.shape[1]
    router_rows = round_up(experts, 16)
    router_cols = round_up(row_dev, 128)
    router_part = jnp.pad(
        w_router.T, ((0, router_rows - experts), (0, router_cols - row_dev))
    )
    packed_all, router_all, full_one = transfer(
        0,
        ("dp", "tensor"),
        [Gather("dp"), Gather("dp"), Gather("tensor")],
        [packed, router_part, normed_one],
        [
            (groups, row_pad, pack_cols),
            (groups, router_rows, router_cols),
            (ranks, tok_dev, width),
        ],
    )
    packed_all = packed_all[:, :row_dev].reshape(width, pack_cols)
    qkv_all, out_all = packed_all[:, : 3 * head_cols], packed_all[:, 3 * head_cols :]
    router_all = jnp.transpose(router_all[:, :experts, :row_dev], (1, 0, 2)).reshape(
        experts, width
    )
    full_one = full_one.reshape(group_tok, width)

    qkv = matmul(full_one, qkv_all).astype(half_type)
    head_out = attend(qkv, lines, seg_rows, seg_cols)
    attn_part = contract_cols(head_out, out_all).astype(half_type)
    mixed = input_f + sum_rows(1, attn_part.reshape(ranks, tok_dev, width))

    gain_two = gain_moe.astype(float_type)
    inv_two = lax.rsqrt(jnp.mean(mixed * mixed, axis=-1, keepdims=True) + EPS)
    unit_two = mixed * inv_two
    normed_two = (unit_two * gain_two).astype(half_type)
    logits = contract_cols(normed_two, router_all)
    router_prob = jax.nn.softmax(logits, axis=-1)
    expert_row = expert_ids[:, 0]
    one_hot = (expert_row[:, None] == jnp.arange(experts, dtype=jnp.int32)[None, :]).astype(
        jnp.int32
    )
    earlier = (places[:, None] > places[None, :]).astype(half_type)
    before = matmul(earlier, one_hot.astype(half_type)).astype(jnp.int32)
    slot_index = jnp.sum(before * one_hot, axis=1)
    destination = expert_row * slots + slot_index
    place_hot = (
        destination[:, None] == jnp.arange(experts * slots, dtype=jnp.int32)[None, :]
    ).astype(half_type)
    own_choice = lax.dynamic_slice_in_dim(one_hot, row_offset, tok_dev, 0).astype(float_type)
    gate_prob = jnp.sum(router_prob * own_choice, axis=1, keepdims=True)
    grad_out = cotangent.astype(float_type)
    grad_y = (gate_prob * grad_out).astype(half_type)

    both = jnp.concatenate(
        [normed_two.reshape(tok_dev, ranks, chunk), grad_y.reshape(tok_dev, ranks, chunk)], axis=2
    )
    both = swap_rows(2, jnp.transpose(both, (1, 0, 2))).reshape(group_tok, 2 * chunk)
    buffer = contract_rows(place_hot, both).astype(half_type)
    returned, grad_w_in, grad_w_out = visit_experts(
        3, buffer.reshape(experts, slots, 2 * chunk), w_in[0], w_out[0]
    )

    returned = returned.reshape(experts * slots, 2 * chunk)
    returned = matmul(place_hot, returned).astype(half_type)
    returned = swap_rows(5, returned.reshape(ranks, tok_dev, 2 * chunk))
    returned = jnp.transpose(returned.reshape(ranks, tok_dev, 2, chunk), (2, 1, 0, 3))
    returned = returned.reshape(2, tok_dev, width).astype(float_type)
    expert_y, grad_norm_two = returned[0], returned[1]
    layer_output = (mixed + gate_prob * expert_y).astype(half_type)
    grad_gate = jnp.sum(grad_out * expert_y, axis=1, keepdims=True)
    grad_logits = (router_prob * (own_choice - gate_prob) * grad_gate).astype(half_type)
    grad_router = contract_rows(grad_logits, normed_two)
    grad_norm_two = grad_norm_two + matmul(grad_logits, router_all)
    gain_two_part = jnp.sum(grad_norm_two * unit_two, axis=0)
    grad_mixed = grad_out + norm_back(grad_norm_two, unit_two, inv_two, gain_two)

    grad_attn = transfer(
        6,
        ("tensor",),
        [Gather("tensor")],
        [grad_mixed.astype(half_type)],
        [(ranks, tok_dev, width)],
    )[0].reshape(group_tok, width)
    grad_out_proj = contract_rows(grad_attn, head_out)
    grad_heads = matmul(grad_attn, out_all).astype(half_type)
    grad_qkv, line_sums = attend_back(qkv, lines, seg_rows, seg_cols, grad_heads)
    sums_hot = jnp.roll(line_hot, group_tok - 1, axis=1).astype(float_type)
    grad_bucket = lax.dot_general(
        line_sums, sums_hot, (((1,), (1,)), ((), ())), precision=lax.Precision.HIGHEST
    )
    grad_full_one = contract_cols(grad_qkv, qkv_all)
    gain_one_part = jnp.sum(grad_full_one * full_one.astype(float_type), axis=0) / gain_one
    grad_weights = jnp.concatenate(
        [contract_rows(full_one, grad_qkv), grad_out_proj], axis=1
    ).astype(half_type)
    grad_weights = jnp.pad(
        grad_weights.reshape(groups, row_dev, pack_cols),
        ((0, 0), (0, row_pad - row_dev), (0, 0)),
    )
    bias_flat = grad_bucket.reshape(1, local_heads * buckets)
    bias_row = jnp.pad(bias_flat, ((0, 0), (0, width - local_heads * buckets)))
    own_rank = (jnp.arange(ranks, dtype=jnp.int32) == tensor_rank).astype(float_type)
    small = jnp.concatenate(
        [gain_one_part[None], gain_two_part[None], own_rank[:, None] * bias_row, grad_router]
    )
    small = jnp.pad(small, ((0, round_up(small.shape[0], 8) - small.shape[0]), (0, 0)))
    grad_norm_one, weight_sums, small_parts = last_sums(
        7, grad_full_one.astype(half_type).reshape(ranks, tok_dev, width), grad_weights, small
    )
    grad_input = grad_mixed + norm_back(grad_norm_one, unit_one, inv_one, gain_one)
    weight_sums = weight_sums[:row_dev]
    small_sums = jnp.sum(small_parts, axis=0)
    router_sum = lax.dynamic_slice(
        small_sums, (2 + ranks, lax.axis_index("dp") * row_dev), (experts, row_dev)
    )
    bias_sum = lax.dynamic_slice_in_dim(small_sums, 2 + tensor_rank, 1, 0)
    bias_sum = bias_sum[0, : local_heads * buckets].reshape(local_heads, buckets)
    return (
        layer_output,
        grad_input,
        small_sums[0],
        small_sums[1],
        weight_sums[:, :head_cols],
        weight_sums[:, head_cols : 2 * head_cols],
        weight_sums[:, 2 * head_cols : 3 * head_cols],
        weight_sums[:, 3 * head_cols :].T,
        router_sum.T,
        bias_sum.T,
        grad_w_in[None],
        grad_w_out[None],
    )


def solution(mesh):
    return jax.shard_map(
        shards,
        mesh=mesh,
        in_specs=(
            P(("dp", "tensor"), None),
            P("dp", None),
            P("dp", None),
            P(),
            P(),
            P(),
            P("dp", "tensor"),
            P("dp", "tensor"),
            P("dp", "tensor"),
            P("tensor", "dp"),
            P("dp", None),
            P(None, "tensor"),
            P("dp", None, "tensor"),
            P("dp", "tensor", None),
            P(("dp", "tensor"), None),
        ),
        out_specs=(
            P(("dp", "tensor"), None),
            P(("dp", "tensor"), None),
            P(),
            P(),
            P("dp", "tensor"),
            P("dp", "tensor"),
            P("dp", "tensor"),
            P("tensor", "dp"),
            P("dp", None),
            P(None, "tensor"),
            P("dp", None, "tensor"),
            P("dp", "tensor", None),
        ),
        check_vma=False,
    )
```

```python
import jax
import jax.numpy as jnp
from jax import lax
from jax.experimental import pallas as pl
from jax.experimental.pallas import tpu as pltpu
from jax.sharding import PartitionSpec as P

DH = 64
EPS = 1e-06
NEG_FILL = -1e30
MESH = pl.DeviceIdType.MESH
VMEM_BYTES = 44 * 1024 * 1024


def round_up(count, unit):
    return (count + unit - 1) // unit * unit


def contract_rows(left, right):
    return lax.dot_general(
        left, right, (((0,), (0,)), ((), ())), preferred_element_type=jnp.float32
    )


def contract_cols(left, right):
    return lax.dot_general(
        left, right, (((1,), (1,)), ((), ())), preferred_element_type=jnp.float32
    )


def matmul(left, right):
    return jnp.dot(left, right, preferred_element_type=jnp.float32)


def norm_back(grad_norm, unit_rows, inv_rms, gain):
    scaled = grad_norm * gain
    return inv_rms * (scaled - unit_rows * jnp.mean(scaled * unit_rows, axis=-1, keepdims=True))


def greet(axes):
    barrier = pltpu.get_barrier_semaphore()
    total = 0
    for axis in axes:
        size = lax.axis_size(axis)
        me = lax.axis_index(axis)
        for shift in range(1, size):
            pl.semaphore_signal(
                barrier,
                inc=1,
                device_id={axis: lax.rem(me + shift, size)},
                device_id_type=MESH,
            )
        total += size - 1
    pl.semaphore_wait(barrier, total)


def push(source, target, sems, slot, axis, peer):
    copy = pltpu.make_async_remote_copy(
        src_ref=source,
        dst_ref=target,
        send_sem=sems.at[(0,) + slot],
        recv_sem=sems.at[(1,) + slot],
        device_id={axis: peer},
        device_id_type=MESH,
    )
    copy.start()
    return copy


def sibling_of(place):
    return place + 1 - 2 * lax.rem(place, 2)


class Swap:
    def __init__(self, axis):
        self.axis = axis

    def sems(self):
        return pltpu.SemaphoreType.DMA((2, lax.axis_size(self.axis)))

    def start(self, source, target, sems):
        size = lax.axis_size(self.axis)
        me = lax.axis_index(self.axis)
        self.copies = []
        for shift in range(1, size):
            peer = lax.rem(me + shift, size)
            self.copies.append(
                push(source.at[peer], target.at[me], sems, (shift,), self.axis, peer)
            )
        target[me] = source[me]

    def middle(self):
        pass

    def finish(self):
        for copy in self.copies:
            copy.wait()


class Gather:
    def __init__(self, axis):
        self.axis = axis

    def sems(self):
        return pltpu.SemaphoreType.DMA((2, 2, lax.axis_size(self.axis) // 2))

    def start(self, source, target, sems):
        size = lax.axis_size(self.axis)
        me = lax.axis_index(self.axis)
        self.target, self.s, self.size, self.me = target, sems, size, me
        self.copies = []
        for shift in range(1, size // 2):
            peer = lax.rem(me + 2 * shift, size)
            self.copies.append(push(source, target.at[me], sems, (0, shift), self.axis, peer))
        self.passed = [push(source, target.at[me], sems, (1, 0), self.axis, sibling_of(me))]
        target[me] = source[...]

    def middle(self):
        for shift in range(1, self.size // 2):
            self.copies[shift - 1].wait_recv()
            origin = lax.rem(self.me + self.size - 2 * shift, self.size)
            block = self.target.at[origin]
            self.passed.append(
                push(block, block, self.s, (1, shift), self.axis, sibling_of(self.me))
            )

    def finish(self):
        for copy in self.copies:
            copy.wait_send()
        for copy in self.passed:
            copy.wait()


class Reduce:
    def __init__(self, axis, shape, dtype):
        self.axis = axis
        self.half = lax.axis_size(axis) // 2
        self.block, self.dtype = tuple(shape), dtype

    def scratch(self):
        slots = pltpu.VMEM((3, self.half) + self.block, self.dtype)
        return [slots, pltpu.SemaphoreType.DMA((2, 2, self.half))]

    def start(self, source, slots, sems):
        self.source, self.slots, self.s = source, slots, sems
        self.size, self.me = lax.axis_size(self.axis), lax.axis_index(self.axis)
        sibling = sibling_of(self.me)
        self.near = {}
        for shift in list(range(1, self.half)) + [0]:
            block = source.at[lax.rem(sibling + 2 * shift, self.size)]
            self.near[shift] = push(
                block, slots.at[0, shift], sems, (0, shift), self.axis, sibling
            )

    def middle(self):
        self.far = {}
        for shift in range(1, self.half):
            self.near[shift].wait_recv()
            peer = lax.rem(self.me + 2 * shift, self.size)
            pair = self.source[peer].astype(jnp.float32)
            pair = pair + self.slots[0, shift].astype(jnp.float32)
            self.slots[1, shift] = pair.astype(self.dtype)
            self.far[shift] = push(
                self.slots.at[1, shift],
                self.slots.at[2, shift],
                self.s,
                (1, shift),
                self.axis,
                peer,
            )

    def finish(self, target):
        self.near[0].wait_recv()
        summed = self.source[self.me].astype(jnp.float32)
        summed = summed + self.slots[0, 0].astype(jnp.float32)
        for shift in range(1, self.half):
            self.far[shift].wait_recv()
            summed = summed + self.slots[2, shift].astype(jnp.float32)
        target[...] = summed
        for copy in list(self.near.values()) + list(self.far.values()):
            copy.wait_send()


def sum_rows(number, operand):
    move = Reduce("tensor", operand.shape[1:], operand.dtype)

    def kernel(source, target, slots, sems):
        greet(("tensor",))
        move.start(source, slots, sems)
        move.middle()
        move.finish(target)

    return pl.pallas_call(
        kernel,
        out_shape=jax.ShapeDtypeStruct(operand.shape[1:], jnp.float32),
        in_specs=[pl.BlockSpec(memory_space=pltpu.VMEM)],
        out_specs=pl.BlockSpec(memory_space=pltpu.VMEM),
        scratch_shapes=move.scratch(),
        compiler_params=pltpu.CompilerParams(
            collective_id=number, has_side_effects=True, vmem_limit_bytes=VMEM_BYTES
        ),
    )(operand)


def transfer(number, axes, moves, operands, shapes):
    count = len(moves)

    def kernel(*refs):
        sources, targets, sems = refs[:count], refs[count : 2 * count], refs[2 * count :]
        greet(axes)
        for move, source, target, sem in zip(moves, sources, targets, sems):
            move.start(source, target, sem)
        for move in moves:
            move.middle()
        for move in moves:
            move.finish()

    return pl.pallas_call(
        kernel,
        out_shape=[jax.ShapeDtypeStruct(s, o.dtype) for s, o in zip(shapes, operands)],
        in_specs=[pl.BlockSpec(memory_space=pltpu.VMEM)] * count,
        out_specs=[pl.BlockSpec(memory_space=pltpu.VMEM)] * count,
        scratch_shapes=[move.sems() for move in moves],
        compiler_params=pltpu.CompilerParams(
            collective_id=number, has_side_effects=True, vmem_limit_bytes=VMEM_BYTES
        ),
    )(*operands)


def swap_rows(number, operand):
    return transfer(number, ("tensor",), [Swap("tensor")], [operand], [operand.shape])[0]


def visit_experts(number, operand, weight_in, weight_out):
    size, slots, columns = operand.shape
    ranks = lax.axis_size("tensor")
    chunk = columns // 2
    width, units = weight_in.shape
    half_type, float_type = jnp.bfloat16, jnp.float32
    steps = min(4, size)
    share = size // steps
    step_rows = share * slots

    def kernel(
        source, w_in, w_out, target, grad_in, grad_out,
        arrived, back, held, pairs, got, total, rows, grads, acts, hids, far, near, home, ret,
    ):
        me, rank = lax.axis_index("dp"), lax.axis_index("tensor")
        across, beside = lax.rem(rank + 2, ranks), sibling_of(rank)
        aslant = lax.rem(beside + 2, ranks)
        groups = [lax.rem(me + size - shift, size) for shift in range(size)]
        greet(("dp", "tensor"))
        arrivals = [None]
        for shift in range(1, size):
            peer = lax.rem(me + shift, size)
            arrivals.append(push(source.at[peer], arrived.at[rank, me], far, (shift,), "dp", peer))
        arrived[rank, me] = source[me]
        first, second, third = {}, {}, {}
        kept, passed, crossed, sent = {}, {}, {}, {}

        def spread(step):
            for shift in range(step * share, (step + 1) * share):
                if shift > 0:
                    arrivals[shift].wait_recv()
                block = arrived.at[rank, groups[shift]]
                first[shift] = push(block, block, near, (0, shift), "tensor", across)
                second[shift] = push(block, block, near, (1, shift), "tensor", beside)

        def relay(step):
            for shift in range(step * share, (step + 1) * share):
                first[shift].wait_recv()
                block = arrived.at[across, groups[shift]]
                third[shift] = push(block, block, near, (2, shift), "tensor", beside)

        def compute(step):
            lo = step * step_rows
            for place in range(share):
                shift = step * share + place
                second[shift].wait_recv()
                third[shift].wait_recv()
                blocks = [arrived[place_t, groups[shift]] for place_t in range(ranks)]
                at = slice(lo + place * slots, lo + (place + 1) * slots)
                rows[at, :] = jnp.concatenate([block[:, :chunk] for block in blocks], axis=1)
                grads[at, :] = jnp.concatenate([block[:, chunk:] for block in blocks], axis=1)
            part = slice(lo, lo + step_rows)
            hidden = matmul(rows[part, :], w_in[...])
            below = 0.5 + 0.5 * lax.erf(hidden * (0.5**0.5))
            slope = below + hidden * jnp.exp(-0.5 * hidden * hidden) * 0.3989422804014327
            activated = (hidden * below).astype(half_type)
            acts[part, :] = activated
            grad_act = contract_cols(grads[part, :], w_out[...])
            grad_hidden = (grad_act * slope).astype(half_type)
            hids[part, :] = grad_hidden
            value = matmul(activated, w_out[...]).astype(half_type)
            grad_rows = contract_cols(grad_hidden, w_in[...]).astype(half_type)
            for place in range(share):
                shift = step * share + place
                at = slice(place * slots, (place + 1) * slots)
                for place_t in range(ranks):
                    cols = slice(place_t * chunk, (place_t + 1) * chunk)
                    back[place_t, groups[shift]] = jnp.concatenate(
                        [value[at, cols], grad_rows[at, cols]], axis=1
                    )

        def pair_up(step):
            for shift in range(step * share, (step + 1) * share):
                group = groups[shift]
                passed[shift] = push(
                    back.at[aslant, group], held.at[1, group], home, (1, shift), "tensor", beside
                )
                kept[shift] = push(
                    back.at[beside, group], held.at[0, group], home, (0, shift), "tensor", beside
                )

        def cross(step):
            for shift in range(step * share, (step + 1) * share):
                group = groups[shift]
                passed[shift].wait_recv()
                pair = back[across, group].astype(float_type) + held[1, group].astype(float_type)
                pairs[group] = pair.astype(half_type)
                crossed[shift] = push(
                    pairs.at[group], got.at[group], home, (2, shift), "tensor", across
                )

        def send_home(step):
            for shift in range(step * share, (step + 1) * share):
                group = groups[shift]
                kept[shift].wait_recv()
                crossed[shift].wait_recv()
                summed = back[rank, group].astype(float_type) + held[0, group].astype(float_type)
                summed = (summed + got[group].astype(float_type)).astype(half_type)
                if shift == 0:
                    target[me] = summed
                else:
                    total[group] = summed
                    sent[shift] = push(
                        total.at[group], target.at[me], ret, (shift,), "dp", group
                    )

        spread(0)
        for step in range(steps):
            relay(step)
            if step + 1 < steps:
                spread(step + 1)
            compute(step)
            pair_up(step)
            if step >= 1:
                cross(step - 1)
            if step >= 2:
                send_home(step - 2)
        if steps >= 2:
            send_home(steps - 2)
        cross(steps - 1)
        grad_out[...] = contract_rows(acts[...], grads[...])
        send_home(steps - 1)
        grad_in[...] = contract_rows(rows[...], hids[...])
        for copy in arrivals[1:]:
            copy.wait_send()
        for copies in (first, second, third, kept, passed, crossed):
            for copy in copies.values():
                copy.wait_send()
        for copy in sent.values():
            copy.wait()

    blocks = (size, slots, columns)
    return pl.pallas_call(
        kernel,
        out_shape=[
            jax.ShapeDtypeStruct(blocks, operand.dtype),
            jax.ShapeDtypeStruct(weight_in.shape, float_type),
            jax.ShapeDtypeStruct(weight_out.shape, float_type),
        ],
        in_specs=[pl.BlockSpec(memory_space=pltpu.VMEM)] * 3,
        out_specs=[pl.BlockSpec(memory_space=pltpu.VMEM)] * 3,
        scratch_shapes=[
            pltpu.VMEM((ranks,) + blocks, half_type),
            pltpu.VMEM((ranks,) + blocks, half_type),
            pltpu.VMEM((2,) + blocks, half_type),
            pltpu.VMEM(blocks, half_type),
            pltpu.VMEM(blocks, half_type),
            pltpu.VMEM(blocks, half_type),
            pltpu.VMEM((size * slots, width), half_type),
            pltpu.VMEM((size * slots, width), half_type),
            pltpu.VMEM((size * slots, units), half_type),
            pltpu.VMEM((size * slots, units), half_type),
            pltpu.SemaphoreType.DMA((2, size)),
            pltpu.SemaphoreType.DMA((2, 3, size)),
            pltpu.SemaphoreType.DMA((2, 3, size)),
            pltpu.SemaphoreType.DMA((2, size)),
        ],
        compiler_params=pltpu.CompilerParams(
            collective_id=number, has_side_effects=True, vmem_limit_bytes=VMEM_BYTES
        ),
    )(operand, weight_in, weight_out)


def last_sums(number, rows, weights, small):
    size, ranks = lax.axis_size("dp"), lax.axis_size("tensor")
    sum_t = Reduce("tensor", rows.shape[1:], rows.dtype)
    sum_d = Reduce("dp", weights.shape[1:], weights.dtype)
    gather_t, gather_d = Gather("tensor"), Gather("dp")

    def kernel(
        rows_in, weights_in, small_in, rows_out, weights_out, small_out,
        held, total, slots_t, sems_t, slots_d, sems_d, sems_g, sems_h,
    ):
        greet(("dp", "tensor"))
        sum_d.start(weights_in, slots_d, sems_d)
        gather_t.start(small_in, held, sems_g)
        sum_t.start(rows_in, slots_t, sems_t)
        gather_t.middle()
        sum_t.middle()
        sum_d.middle()
        gather_t.finish()
        summed = held[0]
        for rank in range(1, ranks):
            summed = summed + held[rank]
        total[...] = summed
        gather_d.start(total, small_out, sems_h)
        sum_t.finish(rows_out)
        gather_d.middle()
        sum_d.finish(weights_out)
        gather_d.finish()

    return pl.pallas_call(
        kernel,
        out_shape=[
            jax.ShapeDtypeStruct(rows.shape[1:], jnp.float32),
            jax.ShapeDtypeStruct(weights.shape[1:], jnp.float32),
            jax.ShapeDtypeStruct((size,) + small.shape, small.dtype),
        ],
        in_specs=[pl.BlockSpec(memory_space=pltpu.VMEM)] * 3,
        out_specs=[pl.BlockSpec(memory_space=pltpu.VMEM)] * 3,
        scratch_shapes=[
            pltpu.VMEM((ranks,) + small.shape, small.dtype),
            pltpu.VMEM(small.shape, small.dtype),
        ]
        + sum_t.scratch()
        + sum_d.scratch()
        + [gather_t.sems(), gather_d.sems()],
        compiler_params=pltpu.CompilerParams(
            collective_id=number, has_side_effects=True, vmem_limit_bytes=VMEM_BYTES
        ),
    )(rows, weights, small)


def head_probs(queries, keys, line, seg_rows, seg_cols):
    tokens = queries.shape[0]
    spread = jnp.broadcast_to(line, (tokens, 2 * tokens))
    bias = pltpu.roll(spread, 0, 1, stride=1, stride_axis=0)[:, :tokens]
    raw = contract_cols(queries, keys) * DH ** (-0.5) + bias
    scores = jnp.where(seg_rows == seg_cols, raw, NEG_FILL)
    expo = jnp.exp(scores - jnp.max(scores, axis=-1, keepdims=True))
    return expo / jnp.sum(expo, axis=-1, keepdims=True)


def attend(qkv, lines, seg_rows, seg_cols):
    tokens, heads = qkv.shape[0], lines.shape[0]
    width = heads * DH

    def kernel(qkv_ref, lines_ref, rows_ref, cols_ref, out_ref):
        parts = []
        for head in range(heads):
            lo = head * DH
            queries = qkv_ref[:, lo : lo + DH]
            keys = qkv_ref[:, width + lo : width + lo + DH]
            values = qkv_ref[:, 2 * width + lo : 2 * width + lo + DH]
            probs = head_probs(
                queries, keys, lines_ref[head : head + 1, :], rows_ref[...], cols_ref[...]
            )
            parts.append(matmul(probs.astype(jnp.bfloat16), values).astype(jnp.bfloat16))
        out_ref[...] = jnp.concatenate(parts, axis=1)

    return pl.pallas_call(
        kernel,
        out_shape=jax.ShapeDtypeStruct((tokens, width), jnp.bfloat16),
        in_specs=[pl.BlockSpec(memory_space=pltpu.VMEM)] * 4,
        out_specs=pl.BlockSpec(memory_space=pltpu.VMEM),
        compiler_params=pltpu.CompilerParams(vmem_limit_bytes=VMEM_BYTES),
    )(qkv, lines, seg_rows, seg_cols)


def attend_back(qkv, lines, seg_rows, seg_cols, grad_heads):
    tokens, heads = qkv.shape[0], lines.shape[0]
    width = heads * DH

    def kernel(qkv_ref, lines_ref, rows_ref, cols_ref, grad_ref, out_ref, sums_ref):
        row = lax.broadcasted_iota(jnp.int32, (tokens, tokens), 0)
        col = lax.broadcasted_iota(jnp.int32, (tokens, tokens), 1)
        flip = (row + col == tokens - 1).astype(jnp.float32).astype(jnp.bfloat16)
        grads_q, grads_k, grads_v = [], [], []
        for head in range(heads):
            lo = head * DH
            queries = qkv_ref[:, lo : lo + DH]
            keys = qkv_ref[:, width + lo : width + lo + DH]
            values = qkv_ref[:, 2 * width + lo : 2 * width + lo + DH]
            grad = grad_ref[:, lo : lo + DH]
            probs = head_probs(
                queries, keys, lines_ref[head : head + 1, :], rows_ref[...], cols_ref[...]
            )
            grads_v.append(contract_rows(probs.astype(jnp.bfloat16), grad))
            grad_probs = contract_cols(grad, values)
            mean = jnp.sum(probs * grad_probs, axis=-1, keepdims=True)
            grad_scores = (probs * (grad_probs - mean)).astype(jnp.bfloat16)
            grads_q.append(matmul(grad_scores, keys) * DH ** (-0.5))
            grads_k.append(contract_rows(grad_scores, queries) * DH ** (-0.5))
            flipped = matmul(flip, grad_scores)
            padded = jnp.concatenate([flipped, jnp.zeros_like(flipped)], axis=1)
            lined = pltpu.roll(padded, 0, 1, stride=1, stride_axis=0)
            sums_ref[head : head + 1, :] = jnp.sum(lined, axis=0, keepdims=True)
        out_ref[...] = jnp.concatenate(grads_q + grads_k + grads_v, axis=1).astype(jnp.bfloat16)

    return pl.pallas_call(
        kernel,
        out_shape=[
            jax.ShapeDtypeStruct((tokens, 3 * width), jnp.bfloat16),
            jax.ShapeDtypeStruct((heads, 2 * tokens), jnp.float32),
        ],
        in_specs=[pl.BlockSpec(memory_space=pltpu.VMEM)] * 5,
        out_specs=[pl.BlockSpec(memory_space=pltpu.VMEM)] * 2,
        compiler_params=pltpu.CompilerParams(vmem_limit_bytes=VMEM_BYTES),
    )(qkv, lines, seg_rows, seg_cols, grad_heads)


def attend_and_sum(number, qkv, lines, seg_rows, seg_cols, out_part, router_part):
    tokens, heads = qkv.shape[0], lines.shape[0]
    width = heads * DH
    size, ranks = lax.axis_size("dp"), lax.axis_size("tensor")
    rows = out_part.shape[0]
    model = size * rows
    half_type = jnp.bfloat16
    block = (tokens // ranks, model)
    move = Reduce("tensor", block, half_type)
    gather_o, gather_r = Gather("dp"), Gather("dp")

    def kernel(
        qkv_ref, lines_ref, rows_ref, cols_ref, out_in, router_in,
        heads_out, sum_out, out_all, router_all, part, slots, sems, sems_o, sems_r,
    ):
        greet(("dp", "tensor"))
        gather_o.start(out_in, out_all, sems_o)
        gather_r.start(router_in, router_all, sems_r)
        parts = []
        for head in range(heads):
            lo = head * DH
            probs = head_probs(
                qkv_ref[:, lo : lo + DH],
                qkv_ref[:, width + lo : width + lo + DH],
                lines_ref[head : head + 1, :],
                rows_ref[...],
                cols_ref[...],
            )
            values = qkv_ref[:, 2 * width + lo : 2 * width + lo + DH]
            parts.append(matmul(probs.astype(half_type), values).astype(half_type))
            if head == 0:
                gather_o.middle()
                gather_r.middle()
        heads_out[...] = jnp.concatenate(parts, axis=1)
        gather_o.finish()
        gather_r.finish()
        projected = contract_cols(heads_out[...], out_all[...].reshape(model, width))
        part[...] = projected.astype(half_type).reshape((ranks,) + block)
        move.start(part, slots, sems)
        move.middle()
        move.finish(sum_out)

    return pl.pallas_call(
        kernel,
        out_shape=[
            jax.ShapeDtypeStruct((tokens, width), half_type),
            jax.ShapeDtypeStruct(block, jnp.float32),
            jax.ShapeDtypeStruct((size,) + out_part.shape, half_type),
            jax.ShapeDtypeStruct((size,) + router_part.shape, half_type),
        ],
        in_specs=[pl.BlockSpec(memory_space=pltpu.VMEM)] * 6,
        out_specs=[pl.BlockSpec(memory_space=pltpu.VMEM)] * 4,
        scratch_shapes=[pltpu.VMEM((ranks,) + block, half_type)]
        + move.scratch()
        + [gather_o.sems(), gather_r.sems()],
        compiler_params=pltpu.CompilerParams(
            collective_id=number, has_side_effects=True, vmem_limit_bytes=VMEM_BYTES
        ),
    )(qkv, lines, seg_rows, seg_cols, out_part, router_part)


def back_and_sum(
    number, qkv, lines, seg_rows, seg_cols, grad_attn, head_out, out_all, full_one, qkv_all,
    sums_hot, small, gain_row,
):
    tokens, heads = qkv.shape[0], lines.shape[0]
    width = heads * DH
    size, ranks = lax.axis_size("dp"), lax.axis_size("tensor")
    model = full_one.shape[1]
    rows = model // size
    buckets = sums_hot.shape[0]
    half_type, float_type = jnp.bfloat16, jnp.float32
    block = (tokens // ranks, model)
    sum_t = Reduce("tensor", block, half_type)
    sum_w = Reduce("dp", (rows, 3 * width), half_type)
    sum_o = Reduce("dp", (rows, width), half_type)
    gather_t, gather_d = Gather("tensor"), Gather("dp")

    def kernel(
        qkv_ref, lines_ref, rows_ref, cols_ref, attn_ref, heads_ref, out_ref, one_ref, all_ref,
        hot_ref, small_ref, gain_ref,
        rows_out, weights_out, proj_out, small_out,
        norm_src, weight_src, proj_src, small_src, held, total,
        slots_t, sems_t, slots_w, sems_w, slots_o, sems_o, sems_g, sems_h,
    ):
        rank = lax.axis_index("tensor")
        greet(("dp", "tensor"))
        grad_proj = contract_rows(attn_ref[...], heads_ref[...]).astype(half_type)
        proj_src[...] = grad_proj.reshape(size, rows, width)
        sum_o.start(proj_src, slots_o, sems_o)
        grad_heads = matmul(attn_ref[...], out_ref[...]).astype(half_type)
        row = lax.broadcasted_iota(jnp.int32, (tokens, tokens), 0)
        col = lax.broadcasted_iota(jnp.int32, (tokens, tokens), 1)
        flip = (row + col == tokens - 1).astype(float_type).astype(half_type)
        grads_q, grads_k, grads_v, sums = [], [], [], []
        for head in range(heads):
            lo = head * DH
            queries = qkv_ref[:, lo : lo + DH]
            keys = qkv_ref[:, width + lo : width + lo + DH]
            values = qkv_ref[:, 2 * width + lo : 2 * width + lo + DH]
            grad = grad_heads[:, lo : lo + DH]
            probs = head_probs(
                queries, keys, lines_ref[head : head + 1, :], rows_ref[...], cols_ref[...]
            )
            grads_v.append(contract_rows(probs.astype(half_type), grad))
            grad_probs = contract_cols(grad, values)
            mean = jnp.sum(probs * grad_probs, axis=-1, keepdims=True)
            grad_scores = (probs * (grad_probs - mean)).astype(half_type)
            grads_q.append(matmul(grad_scores, keys) * DH ** (-0.5))
            grads_k.append(contract_rows(grad_scores, queries) * DH ** (-0.5))
            flipped = matmul(flip, grad_scores)
            padded = jnp.concatenate([flipped, jnp.zeros_like(flipped)], axis=1)
            lined = pltpu.roll(padded, 0, 1, stride=1, stride_axis=0)
            sums.append(jnp.sum(lined, axis=0, keepdims=True))
            if head == 0:
                sum_o.middle()
        grad_qkv = jnp.concatenate(grads_q + grads_k + grads_v, axis=1).astype(half_type)
        grad_weights = contract_rows(one_ref[...], grad_qkv).astype(half_type)
        weight_src[...] = grad_weights.reshape(size, rows, 3 * width)
        sum_w.start(weight_src, slots_w, sems_w)
        grad_one = contract_cols(grad_qkv, all_ref[...])
        norm_src[...] = grad_one.astype(half_type).reshape((ranks,) + block)
        sum_t.start(norm_src, slots_t, sems_t)
        gain_part = jnp.sum(grad_one * one_ref[...].astype(float_type), axis=0, keepdims=True)
        bias = [
            jnp.sum(hot_ref[...] * line, axis=1, keepdims=True) for line in sums
        ]
        lane = lax.broadcasted_iota(jnp.int32, (buckets, model), 1)
        bucket = lax.broadcasted_iota(jnp.int32, (buckets, model), 0)
        spread = jnp.zeros((buckets, model), float_type)
        for head in range(heads):
            spread = spread + jnp.where(lane == bucket + head * buckets, bias[head], 0.0)
        bias_row = jnp.sum(spread, axis=0, keepdims=True)
        small_src[...] = small_ref[...]
        small_src[0:1, :] = gain_part / gain_ref[...]
        for place in range(ranks):
            small_src[2 + place : 3 + place, :] = jnp.where(rank == place, bias_row, 0.0)
        gather_t.start(small_src, held, sems_g)
        sum_t.middle()
        gather_t.middle()
        gather_t.finish()
        summed = held[0]
        for place in range(1, ranks):
            summed = summed + held[place]
        total[...] = summed
        gather_d.start(total, small_out, sems_h)
        sum_w.middle()
        sum_t.finish(rows_out)
        gather_d.middle()
        sum_o.finish(proj_out)
        sum_w.finish(weights_out)
        gather_d.finish()

    return pl.pallas_call(
        kernel,
        out_shape=[
            jax.ShapeDtypeStruct(block, float_type),
            jax.ShapeDtypeStruct((rows, 3 * width), float_type),
            jax.ShapeDtypeStruct((rows, width), float_type),
            jax.ShapeDtypeStruct((size,) + small.shape, float_type),
        ],
        in_specs=[pl.BlockSpec(memory_space=pltpu.VMEM)] * 12,
        out_specs=[pl.BlockSpec(memory_space=pltpu.VMEM)] * 4,
        scratch_shapes=[
            pltpu.VMEM((ranks,) + block, half_type),
            pltpu.VMEM((size, rows, 3 * width), half_type),
            pltpu.VMEM((size, rows, width), half_type),
            pltpu.VMEM(small.shape, float_type),
            pltpu.VMEM((ranks,) + small.shape, float_type),
            pltpu.VMEM(small.shape, float_type),
        ]
        + sum_t.scratch()
        + sum_w.scratch()
        + sum_o.scratch()
        + [gather_t.sems(), gather_d.sems()],
        compiler_params=pltpu.CompilerParams(
            collective_id=number, has_side_effects=True, vmem_limit_bytes=VMEM_BYTES
        ),
    )(
        qkv, lines, seg_rows, seg_cols, grad_attn, head_out, out_all, full_one, qkv_all,
        sums_hot, small, gain_row,
    )


def shards(
    layer_input,
    seq_lengths,
    expert_ids,
    bucket_table,
    gain_attn,
    gain_moe,
    w_query,
    w_key,
    w_value,
    w_attn_out,
    w_router,
    rel_bias,
    w_in,
    w_out,
    cotangent,
):
    float_type = jnp.float32
    half_type = jnp.bfloat16
    tok_dev, width = layer_input.shape
    group_tok = expert_ids.shape[0]
    experts = w_router.shape[1]
    groups, ranks = lax.axis_size("dp"), lax.axis_size("tensor")
    slots = round_up(group_tok // experts + 1, 16)
    local_heads = rel_bias.shape[1]
    head_cols = local_heads * DH
    max_length = (bucket_table.shape[0] + 1) // 2
    buckets = rel_bias.shape[0]
    row_dev = w_query.shape[0]
    row_pad = round_up(row_dev, 16)
    chunk = width // ranks
    tensor_rank = lax.axis_index("tensor")
    row_offset = tensor_rank * tok_dev

    places = jnp.arange(group_tok, dtype=jnp.int32)
    segment = jnp.zeros_like(places)
    start = jnp.zeros((), jnp.int32)
    for sequence in range(seq_lengths.shape[1] - 1):
        start = start + seq_lengths[0, sequence]
        segment = segment + (places >= start).astype(jnp.int32)
    seg_rows, seg_cols = segment[:, None], segment[None, :]
    line_bucket = jnp.concatenate(
        [
            bucket_table[max_length - 1 :],
            jnp.broadcast_to(bucket_table[-1:], (group_tok - max_length,)),
            jnp.broadcast_to(bucket_table[:1], (group_tok - max_length + 1,)),
            bucket_table[: max_length - 1],
        ]
    )
    line_hot = line_bucket[None, :] == jnp.arange(buckets, dtype=jnp.int32)[:, None]
    lines = contract_rows(rel_bias, line_hot.astype(half_type))

    input_f = layer_input.astype(float_type)
    gain_one = gain_attn.astype(float_type)
    inv_one = lax.rsqrt(jnp.mean(input_f * input_f, axis=-1, keepdims=True) + EPS)
    unit_one = input_f * inv_one
    normed_one = (unit_one * gain_one).astype(half_type)
    whole_rows = row_pad == row_dev
    packed = [w_query, w_key, w_value] if whole_rows else [w_query, w_key, w_value, w_attn_out.T]
    packed = jnp.concatenate(packed, axis=1)
    packed = jnp.pad(packed, ((0, row_pad - row_dev), (0, 0)))
    pack_cols = packed.shape[1]
    router_rows = round_up(experts, 16)
    router_cols = round_up(row_dev, 128)
    router_part = jnp.pad(
        w_router.T, ((0, router_rows - experts), (0, router_cols - row_dev))
    )
    early = [] if whole_rows else [router_part]
    gathered = transfer(
        0,
        ("dp", "tensor"),
        [Gather("dp")] + [Gather("dp") for _ in early] + [Gather("tensor")],
        [packed] + early + [normed_one],
        [(groups, row_pad, pack_cols)]
        + [(groups, router_rows, router_cols) for _ in early]
        + [(ranks, tok_dev, width)],
    )
    packed_all = gathered[0][:, :row_dev].reshape(width, pack_cols)
    qkv_all = packed_all[:, : 3 * head_cols]
    full_one = gathered[-1].reshape(group_tok, width)

    qkv = matmul(full_one, qkv_all).astype(half_type)
    if whole_rows:
        head_out, attn_rows, out_all, router_all = attend_and_sum(
            1, qkv, lines, seg_rows, seg_cols, w_attn_out.T, router_part
        )
        out_all = out_all.reshape(width, head_cols)
    else:
        out_all, router_all = packed_all[:, 3 * head_cols :], gathered[1]
        head_out = attend(qkv, lines, seg_rows, seg_cols)
        attn_part = contract_cols(head_out, out_all).astype(half_type)
        attn_rows = sum_rows(1, attn_part.reshape(ranks, tok_dev, width))
    router_all = jnp.transpose(router_all[:, :experts, :row_dev], (1, 0, 2)).reshape(
        experts, width
    )
    mixed = input_f + attn_rows

    gain_two = gain_moe.astype(float_type)
    inv_two = lax.rsqrt(jnp.mean(mixed * mixed, axis=-1, keepdims=True) + EPS)
    unit_two = mixed * inv_two
    normed_two = (unit_two * gain_two).astype(half_type)
    logits = contract_cols(normed_two, router_all)
    router_prob = jax.nn.softmax(logits, axis=-1)
    expert_row = expert_ids[:, 0]
    one_hot = (expert_row[:, None] == jnp.arange(experts, dtype=jnp.int32)[None, :]).astype(
        jnp.int32
    )
    earlier = (places[:, None] > places[None, :]).astype(half_type)
    before = matmul(earlier, one_hot.astype(half_type)).astype(jnp.int32)
    slot_index = jnp.sum(before * one_hot, axis=1)
    destination = expert_row * slots + slot_index
    place_hot = (
        destination[:, None] == jnp.arange(experts * slots, dtype=jnp.int32)[None, :]
    ).astype(half_type)
    own_choice = lax.dynamic_slice_in_dim(one_hot, row_offset, tok_dev, 0).astype(float_type)
    gate_prob = jnp.sum(router_prob * own_choice, axis=1, keepdims=True)
    grad_out = cotangent.astype(float_type)
    grad_y = (gate_prob * grad_out).astype(half_type)

    both = jnp.concatenate(
        [normed_two.reshape(tok_dev, ranks, chunk), grad_y.reshape(tok_dev, ranks, chunk)], axis=2
    )
    both = swap_rows(2, jnp.transpose(both, (1, 0, 2))).reshape(group_tok, 2 * chunk)
    buffer = contract_rows(place_hot, both).astype(half_type)
    returned, grad_w_in, grad_w_out = visit_experts(
        3, buffer.reshape(experts, slots, 2 * chunk), w_in[0], w_out[0]
    )

    returned = returned.reshape(experts * slots, 2 * chunk)
    returned = matmul(place_hot, returned).astype(half_type)
    returned = swap_rows(5, returned.reshape(ranks, tok_dev, 2 * chunk))
    returned = jnp.transpose(returned.reshape(ranks, tok_dev, 2, chunk), (2, 1, 0, 3))
    returned = returned.reshape(2, tok_dev, width).astype(float_type)
    expert_y, grad_norm_two = returned[0], returned[1]
    layer_output = (mixed + gate_prob * expert_y).astype(half_type)
    grad_gate = jnp.sum(grad_out * expert_y, axis=1, keepdims=True)
    grad_logits = (router_prob * (own_choice - gate_prob) * grad_gate).astype(half_type)
    grad_router = contract_rows(grad_logits, normed_two)
    grad_norm_two = grad_norm_two + matmul(grad_logits, router_all)
    gain_two_part = jnp.sum(grad_norm_two * unit_two, axis=0)
    grad_mixed = grad_out + norm_back(grad_norm_two, unit_two, inv_two, gain_two)

    grad_attn = transfer(
        6,
        ("tensor",),
        [Gather("tensor")],
        [grad_mixed.astype(half_type)],
        [(ranks, tok_dev, width)],
    )[0].reshape(group_tok, width)
    sums_hot = jnp.roll(line_hot, group_tok - 1, axis=1).astype(float_type)
    if whole_rows:
        small = jnp.concatenate(
            [
                jnp.zeros((1, width), float_type),
                gain_two_part[None],
                jnp.zeros((ranks, width), float_type),
                grad_router,
            ]
        )
        small = jnp.pad(small, ((0, round_up(small.shape[0], 8) - small.shape[0]), (0, 0)))
        grad_norm_one, weight_sums, proj_sums, small_parts = back_and_sum(
            7, qkv, lines, seg_rows, seg_cols, grad_attn, head_out, out_all, full_one, qkv_all,
            sums_hot, small, gain_one[None],
        )
    else:
        grad_out_proj = contract_rows(grad_attn, head_out)
        grad_heads = matmul(grad_attn, out_all).astype(half_type)
        grad_qkv, line_sums = attend_back(qkv, lines, seg_rows, seg_cols, grad_heads)
        grad_bucket = lax.dot_general(
            line_sums, sums_hot, (((1,), (1,)), ((), ())), precision=lax.Precision.HIGHEST
        )
        grad_full_one = contract_cols(grad_qkv, qkv_all)
        gain_one_part = jnp.sum(grad_full_one * full_one.astype(float_type), axis=0) / gain_one
        grad_weights = jnp.concatenate(
            [contract_rows(full_one, grad_qkv), grad_out_proj], axis=1
        ).astype(half_type)
        grad_weights = jnp.pad(
            grad_weights.reshape(groups, row_dev, pack_cols),
            ((0, 0), (0, row_pad - row_dev), (0, 0)),
        )
        bias_flat = grad_bucket.reshape(1, local_heads * buckets)
        bias_row = jnp.pad(bias_flat, ((0, 0), (0, width - local_heads * buckets)))
        own_rank = (jnp.arange(ranks, dtype=jnp.int32) == tensor_rank).astype(float_type)
        small = jnp.concatenate(
            [gain_one_part[None], gain_two_part[None], own_rank[:, None] * bias_row, grad_router]
        )
        small = jnp.pad(small, ((0, round_up(small.shape[0], 8) - small.shape[0]), (0, 0)))
        grad_norm_one, weight_sums, small_parts = last_sums(
            7, grad_full_one.astype(half_type).reshape(ranks, tok_dev, width), grad_weights, small
        )
    grad_input = grad_mixed + norm_back(grad_norm_one, unit_one, inv_one, gain_one)
    if not whole_rows:
        weight_sums = weight_sums[:row_dev]
        proj_sums = weight_sums[:, 3 * head_cols :]
    small_sums = jnp.sum(small_parts, axis=0)
    router_sum = lax.dynamic_slice(
        small_sums, (2 + ranks, lax.axis_index("dp") * row_dev), (experts, row_dev)
    )
    bias_sum = lax.dynamic_slice_in_dim(small_sums, 2 + tensor_rank, 1, 0)
    bias_sum = bias_sum[0, : local_heads * buckets].reshape(local_heads, buckets)
    return (
        layer_output,
        grad_input,
        small_sums[0],
        small_sums[1],
        weight_sums[:, :head_cols],
        weight_sums[:, head_cols : 2 * head_cols],
        weight_sums[:, 2 * head_cols : 3 * head_cols],
        proj_sums.T,
        router_sum.T,
        bias_sum.T,
        grad_w_in[None],
        grad_w_out[None],
    )


def solution(mesh):
    return jax.shard_map(
        shards,
        mesh=mesh,
        in_specs=(
            P(("dp", "tensor"), None),
            P("dp", None),
            P("dp", None),
            P(),
            P(),
            P(),
            P("dp", "tensor"),
            P("dp", "tensor"),
            P("dp", "tensor"),
            P("tensor", "dp"),
            P("dp", None),
            P(None, "tensor"),
            P("dp", None, "tensor"),
            P("dp", "tensor", None),
            P(("dp", "tensor"), None),
        ),
        out_specs=(
            P(("dp", "tensor"), None),
            P(("dp", "tensor"), None),
            P(),
            P(),
            P("dp", "tensor"),
            P("dp", "tensor"),
            P("dp", "tensor"),
            P("tensor", "dp"),
            P("dp", None),
            P(None, "tensor"),
            P("dp", None, "tensor"),
            P("dp", "tensor", None),
        ),
        check_vma=False,
    )
```
